128 devices in a mesh: gx: 8 (over x, z_lo), gy: 16 (over z_hi, y, core).
Axes of the slice: x: 4, y: 4, z: 4 (z_hi: 2, z_lo: 2; z = z_hi * 2 + z_lo), core: 2. Of those that a mesh axis runs over, the one named last changes fastest.
Arguments:
- displacement: float32 [2, 3, 8, 1024, 2048], P(None, None, None, 'gx', 'gy'), may hold values from -0.6 to 0.6
- velocity: float32 [2, 3, 8, 1024, 2048], P(None, None, None, 'gx', 'gy'), may hold values from -3 to 3
- modulus: float32 [2, 8, 1024, 2048], P(None, None, 'gx', 'gy'), may hold values from 0.5 to 2
- density: float32 [2, 8, 1024, 2048], P(None, None, 'gx', 'gy'), may hold values from 1 to 4
- clearance: float32 [1024, 2048], P('gx', 'gy'), may hold values from -0.3 to 0.3
- mortar_coupling: float32 [128, 128], replicated, may hold values from -0.5 to 0.5
- pair_owner: int32 [8, 4096, 1], P('gx', 'gy'), may hold values from 0 to 15; in each aligned block of 256 rows (0 to 255, 256 to 511, ..., all dimensions but the last counted through in order) at most 64 rows name the same one
- pair_row: int32 [8, 4096, 1], P('gx', 'gy'), may hold values from 0 to 127
- pair_offset: int32 [8, 4096, 1], P('gx', 'gy'), may hold values from 0 to 127
- pair_active: int32 [8, 4096, 1], P('gx', 'gy'), may hold values 0 or 1
Outputs:
- new_displacement: float32 [2, 3, 8, 1024, 2048], P(None, None, None, 'gx', 'gy')
- new_velocity: float32 [2, 3, 8, 1024, 2048], P(None, None, None, 'gx', 'gy')
The draws below stay inside these ranges and needn't reach their ends.
Inputs may be any that keep to these rules, and one draw needn't show every extreme that they name: `pair_owner`: in the pairs of one device, at most 64 name one owner, and one owner is named by exactly 64 pairs of some device.
All inputs are finite; a program needn't handle non-finite values. No bound on the sum of `pair_active` on one device may be relied on, other than what follows from the above.
Results may differ from the reference program's by a relative error of at most 0.0001.
Values sent between devices are 32-bit elements; how exact they have to be, the bound alone decides.
A program may use at most 192 MiB of HBM per device.

```python
import math
import jax
import jax.numpy as jnp
import numpy as np
from jax import lax

CX = 128
TILE = 128
LAYERS = 8
INTERSECTIONS = 2
STEPS = 2
NX = 1024
NY = 2048
PAIRS = 256
CAP = 64
N_GX = 8
N_GY = 16


def plant(entries, rng, least, largest):
    shape = entries.shape
    spot = [jax.random.randint(jax.random.fold_in(rng, axis), (), 0, shape[axis]) for axis in range(len(shape))]
    entries = entries.at[tuple(spot)].set(least)
    longest = shape.index(max(shape))
    spot[longest] = (spot[longest] + 1) % shape[longest]
    return entries.at[tuple(spot)].set(largest)


def levels(own_key, dims, split, smallest, high):
    def one(dim, blocks):
        heights = jax.random.uniform(jax.random.fold_in(jax.random.fold_in(own_key, 6), dim), (blocks,), jnp.float32, smallest / len(split), high / len(split))
        return jnp.repeat(jnp.exp(heights), dims[dim] // blocks).reshape((-1,) + (1,) * (len(dims) - dim - 1))

    gain = one(*split[0])
    for cut in split[1:]:
        gain = gain * one(*cut)
    return gain


def deal_out(own_key, own, number, rows, count, top, reach, skew):
    sequence = jax.random.permutation(own_key, count)
    packed, usual = shares(count, rows * top, reach, skew, True), shares(count, rows * top, reach, skew, False)
    places = jnp.arange(count)

    def named(sizes, turn):
        used = int((sizes > 0).sum())
        fixed = max(1, used // 4)
        passed = fixed + (places - fixed + turn * (used - fixed)) % max(1, count - fixed)
        return jnp.zeros((count,), jnp.int32).at[sequence[jnp.where(places < fixed, places, passed)]].set(jnp.asarray(sizes, jnp.int32))

    sizes = jnp.where(number % 4 == 0, named(packed, number // 4), named(usual, number - number // 4 - 1))
    mixed = jax.random.permutation(jax.random.fold_in(own, 3), count)
    source_of, sink = mixed[0:count // 2 * 2:2], mixed[1:count // 2 * 2:2]
    slack = jnp.minimum(sizes[source_of] - 1, reach - sizes[sink]) // 2
    slack = jnp.where((source_of == sequence[0]) | (sink == sequence[0]) | (sizes[sink] == 0), 0, jnp.maximum(slack, 0))
    passed = jax.random.randint(jax.random.fold_in(own, 4), (count // 2,), 0, 1 << 20) % (slack + 1)
    sizes = sizes.at[source_of].add(-passed).at[sink].add(passed)
    labels = jnp.searchsorted(jnp.cumsum(sizes), jnp.arange(rows * top), side="right").astype(jnp.int32)
    listing = labels.reshape(top, rows).T
    listing = listing[jax.random.permutation(jax.random.fold_in(own, 1), rows)]
    turn = jax.random.randint(jax.random.fold_in(own, 2), (rows, 1), 0, top)
    return jnp.take_along_axis(listing, (jnp.arange(top)[None, :] + turn) % top, axis=1)


def shares(amount, total, bound, skew, full):
    loads = [(1 << 20) // math.isqrt(grade ** skew) + 1 for grade in range(1, amount + 1)]
    largest = bound if full else min(bound, max(-(-total // amount), total * loads[0] // sum(loads)))
    least = 1 if total - largest >= amount - 1 else 0
    counts, spare = [largest] + [least] * (amount - 1), total - largest - least * (amount - 1)
    while spare > 0:
        movable = [i for i in range(1, amount) if counts[i] < largest] or [i for i in range(1, amount) if counts[i] < bound]
        whole, left = sum([loads[i] for i in movable]), spare
        for i in movable:
            addition = min(bound - counts[i], max(1, left * loads[i] // whole), spare)
            counts[i] = counts[i] + addition
            spare = spare - addition
    return np.array(counts)


def centred(stream_key, dims, deviation, bound, split=(), kind=jnp.bfloat16):
    result = jax.random.normal(stream_key, dims, jnp.float32) * deviation
    if len(split) > 0:
        result = levels(stream_key, dims, split, -0.22, 0.18) * result
    return jnp.clip(result, min=-bound, max=bound).astype(kind)


def setup_inputs(seed: int = 0) -> dict:
    splits = jax.random.split(jax.random.key(seed), 11)
    displacement = centred(splits[0], (2, 3, LAYERS, NX, NY), 0.1, 0.6, ((3, 8), (4, 16)), jnp.float32)
    velocity = centred(splits[1], (2, 3, LAYERS, NX, NY), 0.5, 3.0, ((3, 8), (4, 16)), jnp.float32)
    modulus = jnp.clip(jnp.exp(math.log(2.0) - 1.3862944 * jax.random.uniform(splits[2], (2, LAYERS, NX, NY), jnp.float32) ** levels(splits[2], (2, LAYERS, NX, NY), ((2, 8), (3, 16)), -0.2, 0.2)), 0.5, 2.0)
    density = jnp.clip(jnp.exp(math.log(4.0) - 1.3862944 * jax.random.uniform(splits[3], (2, LAYERS, NX, NY), jnp.float32) ** levels(splits[3], (2, LAYERS, NX, NY), ((2, 8), (3, 16)), -0.2, 0.2)), 1.0, 4.0)
    clearance = jnp.clip(jax.random.uniform(splits[4], (NX, NY), jnp.float32, -0.3, 0.3) * levels(splits[4], (NX, NY), ((0, 8), (1, 16)), -0.4, 0.0), -0.3, 0.3)
    mortar_coupling = centred(splits[5], (TILE, TILE), TILE ** -0.5, 0.5, (), jnp.float32)
    pair_owner_keys = jax.random.split(jax.random.fold_in(splits[6], 1), N_GX * (N_GY * PAIRS) // PAIRS)
    pair_owner_turns = jax.random.permutation(jax.random.fold_in(splits[6], 3), N_GX * (N_GY * PAIRS) // PAIRS)
    pair_owner = jax.vmap(lambda own, number: deal_out(jax.random.fold_in(splits[6], 2), own, number, PAIRS, N_GY, 1, CAP, 2))(pair_owner_keys, pair_owner_turns).reshape((N_GX, N_GY * PAIRS, 1))
    pair_row = plant(jax.random.randint(splits[7], (N_GX, N_GY * PAIRS, 1), 0, CX), jax.random.fold_in(splits[7], 1), 0, CX - 1).astype(jnp.int32)
    pair_offset = plant(jax.random.randint(splits[8], (N_GX, N_GY * PAIRS, 1), 0, TILE), jax.random.fold_in(splits[8], 1), 0, TILE - 1).astype(jnp.int32)
    pair_active = plant((jax.random.randint(splits[9], (N_GX, N_GY * PAIRS, 1), 0, 4) < 3).astype(jnp.int32), jax.random.fold_in(splits[9], 1), 0, 1)
    return {"displacement": displacement, "velocity": velocity, "modulus": modulus, "density": density, "clearance": clearance, "mortar_coupling": mortar_coupling, "pair_owner": pair_owner, "pair_row": pair_row, "pair_offset": pair_offset, "pair_active": pair_active}


time_step = 0.2
penalty_stiffness = 4.0


def internal_force(padded_disp, padded_mod, layers, xcount, ycount):
    centre_disp = padded_disp[:, :, 1:1 + layers, 1:1 + xcount, 1:1 + ycount]
    centre_mod = padded_mod[:, 1:1 + layers, 1:1 + xcount, 1:1 + ycount]
    stencil_sum = jnp.zeros_like(centre_disp)
    for depth_step in (-1, 0, 1):
        for row_step in (-1, 0, 1):
            for col_step in (-1, 0, 1):
                nonzero = abs(depth_step) + abs(row_step) + abs(col_step)
                if nonzero == 0:
                    continue
                weight_value = 0.5 ** (nonzero - 1)
                near_mod = padded_mod[:, 1 + depth_step:1 + depth_step + layers, 1 + row_step:1 + row_step + xcount, 1 + col_step:1 + col_step + ycount]
                near_disp = padded_disp[:, :, 1 + depth_step:1 + depth_step + layers, 1 + row_step:1 + row_step + xcount, 1 + col_step:1 + col_step + ycount]
                coupling = weight_value * 2.0 * centre_mod * near_mod / (centre_mod + near_mod)
                stencil_sum = stencil_sum + coupling[:, None] * (near_disp - centre_disp)
    return stencil_sum


def reference(displacement, velocity, modulus, density, clearance, mortar_coupling, pair_owner, pair_row, pair_offset, pair_active):
    owners = pair_owner[..., 0].reshape(N_GX, N_GY, PAIRS).astype(jnp.int32)
    row_ids = pair_row[..., 0].reshape(N_GX, N_GY, PAIRS).astype(jnp.int32)
    offsets = pair_offset[..., 0].reshape(N_GX, N_GY, PAIRS).astype(jnp.int32)
    active_weight = pair_active[..., 0].reshape(N_GX, N_GY, PAIRS).astype(jnp.float32)
    gx_index = jnp.arange(N_GX, dtype=jnp.int32)[:, None, None]
    gy_index = jnp.arange(N_GY, dtype=jnp.int32)[None, :, None]
    slave_tile = (jnp.arange(PAIRS, dtype=jnp.int32) // INTERSECTIONS)[None, None, :]
    lane_ids = jnp.arange(TILE, dtype=jnp.int32)
    forward_index = (lane_ids[None, None, None, :] + offsets[..., None]) % TILE
    backward_index = (lane_ids[None, None, None, :] - offsets[..., None] + TILE) % TILE
    clear_tiles = clearance.reshape(N_GX, CX, N_GY, TILE)[gx_index, slave_tile, gy_index]
    padded_mod = jnp.pad(modulus, ((0, 0), (1, 1), (1, 1), (1, 1)))
    for step_count in range(STEPS):
        padded_disp = jnp.pad(displacement, ((0, 0), (0, 0), (1, 1), (1, 1), (1, 1)))
        net_force = internal_force(padded_disp, padded_mod, LAYERS, NX, NY)
        master_face = displacement[0, 2, 0].reshape(N_GX, CX, N_GY, TILE)
        slave_face = displacement[1, 2, 0].reshape(N_GX, CX, N_GY, TILE)
        master_rows = master_face[gx_index, row_ids, owners]
        shifted = jnp.take_along_axis(master_rows, forward_index, axis=3)
        projected = shifted + jnp.einsum("abpj,jk->abpk", shifted, mortar_coupling, precision=lax.Precision.HIGHEST)
        gap_width = clear_tiles + slave_face[gx_index, slave_tile, gy_index] - projected
        traction = penalty_stiffness * active_weight[..., None] * jnp.maximum(0.0, -gap_width)
        back_proj = traction + jnp.einsum("abpk,jk->abpj", traction, mortar_coupling, precision=lax.Precision.HIGHEST)
        master_part = jnp.take_along_axis(back_proj, backward_index, axis=3)
        master_force = jnp.zeros((N_GX, CX, N_GY, TILE), jnp.float32).at[gx_index, row_ids, owners].add(master_part)
        slave_force = jnp.zeros((N_GX, CX, N_GY, TILE), jnp.float32).at[gx_index, slave_tile, gy_index].add(traction)
        net_force = net_force.at[0, 2, 0].add(-master_force.reshape(NX, NY))
        net_force = net_force.at[1, 2, 0].add(slave_force.reshape(NX, NY))
        velocity = velocity + time_step * net_force / density[:, None]
        displacement = displacement + time_step * velocity
    return displacement, velocity
```

```python
import functools

import jax
import jax.numpy as jnp
from jax import lax
from jax.experimental import pallas as pl
from jax.experimental.pallas import tpu as pltpu
from jax.sharding import PartitionSpec as P

STEPS = 2
LAYERS = 8
TILE = 128
BLOCKS = TILE // 8
PAIRS = 256
GROUPS = 6
MASTER, SLAVE = 2, 5
LOW, MAIN, HIGH = 7, 8, 136

time_step = 0.2
penalty_stiffness = 4.0

MESH = pl.DeviceIdType.MESH
f32 = jnp.float32


def lanes(shape):
    return lax.broadcasted_iota(jnp.int32, shape, len(shape) - 1)


def cyclic_shift(values, offsets, direction):
    for bit in range(7):
        amount = 1 << bit
        rolled = pltpu.roll(values, (direction * amount) % TILE, axis=1)
        values = jnp.where((offsets & amount) != 0, rolled, values)
    return values


def kernel(
    n_gx, n_gy,
    disp, vel, mod, dens, clear, mortar, flat_s, pair_v,
    u_out, v_out,
    U, V, D, L, C, FACES, T, RP, RR, OH, XS, YS, HX, HY, HD, OFFS, ACT, SL, SF, ROWS, DINV,
    load_sem, own_sem, halo_send, halo_recv, face_send, face_recv, pass_send, pass_recv,
    core_send, core_recv, sum_send, sum_recv, store_sem,
):
    gx = lax.axis_index("gx")
    gy = lax.axis_index("gy")
    core = lax.rem(gy, 2)
    chip = gy // 2
    chips = n_gy // 2
    partner = gy + 1 - 2 * core
    up = lax.rem(gx + n_gx - 1, n_gx)
    down = lax.rem(gx + 1, n_gx)
    left = lax.rem(gy + n_gy - 1, n_gy)
    right = lax.rem(gy + 1, n_gy)
    other = lax.rem(gy + n_gy - 1 + 2 * core, n_gy)

    def at(x, y):
        return {"gx": x, "gy": y}

    def mate(q):
        return 2 * lax.rem(chip + q, chips) + core

    loads = [
        pltpu.make_async_copy(disp, U.at[pl.ds(0, GROUPS)], load_sem.at[0]),
        pltpu.make_async_copy(mod, U.at[pl.ds(GROUPS, 2)], load_sem.at[1]),
        pltpu.make_async_copy(dens, D, load_sem.at[2]),
        pltpu.make_async_copy(vel, V, load_sem.at[3]),
    ]
    for load in loads:
        load.start()

    barrier = pltpu.get_barrier_semaphore()
    friends = [at(gx, mate(q)) for q in range(1, chips)]
    friends += [at(gx, partner), at(gx, other)]
    friends += [at(x, y) for x in (up, down) for y in (left, gy, right)]
    for friend in friends:
        pl.semaphore_signal(barrier, inc=1, device_id=friend, device_id_type=MESH)
    pl.semaphore_wait(barrier, len(friends))

    def remote(src, dst, send, recv, target):
        return pltpu.make_async_remote_copy(
            src_ref=src, dst_ref=dst, send_sem=send, recv_sem=recv,
            device_id=target, device_id_type=MESH,
        )

    def block_of(j):
        return pl.ds(pl.multiple_of(j * TILE, TILE), TILE)

    def face_copies(step, src):
        mine = FACES.at[step, block_of(gy)]
        out = [remote(src, mine, face_send.at[step, 0], face_recv.at[step, 0], at(gx, partner))]
        for q in range(1, chips):
            out.append(remote(src, mine, face_send.at[step, q], face_recv.at[step, q], at(gx, mate(q))))
        return out

    def pass_copy(step, q):
        held = FACES.at[step, block_of(mate(chips - q))]
        return remote(held, held, pass_send.at[step, q], pass_recv.at[step, q], at(gx, partner))

    def send_faces(step, src):
        copies = face_copies(step, src)
        for q in [1, chips - 1] + list(range(2, chips - 1)) + [0]:
            copies[q].start()
        own = pltpu.make_async_copy(src, FACES.at[step, block_of(gy)], own_sem.at[step])
        own.start()
        return copies, own

    def finish_faces(step, copies, own):
        passed = []
        for q in [1, chips - 1] + list(range(2, chips - 1)):
            copies[q].wait_recv()
            copy = pass_copy(step, q)
            copy.start()
            passed.append(copy)
        own.wait()
        copies[0].wait_recv()
        for copy in passed:
            copy.wait_recv()
        for copy in copies + passed:
            copy.wait_send()

    def pack(groups):
        def one(g, carry):
            lane = lanes((8, TILE))

            def layer(l, both):
                low, high = both
                for t in range(BLOCKS):
                    spot = l * BLOCKS + t
                    r = pltpu.roll(U[g, l, t * 8 : t * 8 + 8, :], lax.rem(spot + 1, TILE), axis=1)
                    high = jnp.where(lane == spot, r, high)
                    low = jnp.where(lane == lax.rem(spot + 1, TILE), r, low)
                row = g * 8 + l
                XS[0, pl.ds(row, 1), :] = U[g, l, 0:1, :]
                XS[1, pl.ds(row, 1), :] = U[g, l, TILE - 1 : TILE, :]
                return low, high

            zero = jnp.zeros((8, TILE), f32)
            low, high = lax.fori_loop(0, LAYERS, layer, (zero, zero))
            rows = pl.ds(pl.multiple_of(g * 8, 8), 8)
            YS[0, rows, :] = low
            YS[1, rows, :] = high
            return carry

        lax.fori_loop(0, groups, one, 0)

    def halo_copies(step, groups):
        rows = pl.ds(0, groups * 8)
        plan = [
            (XS.at[0, rows], HX.at[step, 1, rows], at(up, gy)),
            (XS.at[1, rows], HX.at[step, 0, rows], at(down, gy)),
            (YS.at[0, rows], HY.at[step, 1, rows], at(gx, left)),
            (YS.at[1, rows], HY.at[step, 0, rows], at(gx, right)),
            (XS.at[0, rows], HD.at[step, 3, rows], at(up, left)),
            (XS.at[0, rows], HD.at[step, 2, rows], at(up, right)),
            (XS.at[1, rows], HD.at[step, 1, rows], at(down, left)),
            (XS.at[1, rows], HD.at[step, 0, rows], at(down, right)),
        ]
        return [
            remote(src, dst, halo_send.at[step, k], halo_recv.at[step, k], target)
            for k, (src, dst, target) in enumerate(plan)
        ]

    def spread(step, first, groups):
        at_top = (gx == 0).astype(f32)
        at_bottom = (gx == n_gx - 1).astype(f32)
        at_left = (gy == 0).astype(f32)
        at_right = (gy == n_gy - 1).astype(f32)

        def one(g, carry):
            is_mod = (g >= GROUPS).astype(f32)
            keep_top, keep_bottom = 1.0 - is_mod * at_top, 1.0 - is_mod * at_bottom
            keep_left, keep_right = 1.0 - is_mod * at_left, 1.0 - is_mod * at_right
            lane = lanes((8, TILE))
            rows = pl.ds(pl.multiple_of(g * 8, 8), 8)
            low = HY[step, 0, rows, :] * keep_left
            high = HY[step, 1, rows, :] * keep_right

            def layer(l, carry):
                for t in range(BLOCKS):
                    turn = TILE - 1 - (l * BLOCKS + t)
                    here = U[g, l, t * 8 : t * 8 + 8, :]
                    after = jnp.where(lane == 0, pltpu.roll(high, turn, axis=1), here)
                    before = jnp.where(lane == TILE - 1, pltpu.roll(low, turn, axis=1), here)
                    into = slice(MAIN + t * 8, MAIN + t * 8 + 8)
                    L[0, g, l, into, :] = pltpu.roll(before, 1, axis=1)
                    L[1, g, l, into, :] = here
                    L[2, g, l, into, :] = pltpu.roll(after, TILE - 1, axis=1)
                return carry

            lax.fori_loop(0, LAYERS, layer, 0)
            for side, keep, spot in ((0, keep_top, LOW), (1, keep_bottom, HIGH)):
                here = HX[step, side, rows, :] * keep
                corner_low = HD[step, 2 * side, rows, :] * (keep * keep_left)
                corner_high = HD[step, 2 * side + 1, rows, :] * (keep * keep_right)
                before = pltpu.roll(jnp.where(lane == TILE - 1, corner_low, here), 1, axis=1)
                after = pltpu.roll(jnp.where(lane == 0, corner_high, here), TILE - 1, axis=1)
                for dy, plane in enumerate((before, here, after)):
                    for l in range(LAYERS):
                        L[dy, g, l, spot : spot + 1, :] = plane[l : l + 1, :]
            return carry

        lax.fori_loop(first, first + groups, one, 0)

    def couplings():
        def one(it, carry):
            b = it // (BLOCKS * LAYERS)
            t = lax.rem(it // LAYERS, BLOCKS)
            l = lax.rem(it, LAYERS)
            row = pl.multiple_of(t * 8, 8)
            own = L[1, GROUPS + b, l, pl.ds(row + MAIN, 8), :]
            base = own * (time_step / D[b, l, pl.ds(row, 8), :])
            total = jnp.zeros((8, TILE), f32)
            for dl in (-1, 0, 1):
                near = jnp.clip(l + dl, 0, LAYERS - 1)
                inside = jnp.logical_and(l + dl >= 0, l + dl < LAYERS).astype(f32)
                scaled = base if dl == 0 else base * inside
                for dx in (-1, 0, 1):
                    for dy in (-1, 0, 1):
                        nonzero = abs(dl) + abs(dx) + abs(dy)
                        if nonzero == 0:
                            continue
                        e = L[dy + 1, GROUPS + b, near, pl.ds(row + MAIN + dx, 8), :]
                        weight = 2.0 * 0.5 ** (nonzero - 1)
                        c = (scaled * weight) * (e / (own + e))
                        C[b * BLOCKS + t, l, (dl + 1) * 9 + (dx + 1) * 3 + dy + 1] = c
                        total = total + c
            C[b * BLOCKS + t, l, 13] = -total
            return carry

        lax.fori_loop(0, 2 * BLOCKS * LAYERS, one, 0)

    def advance():
        def one(it, carry):
            b = it // BLOCKS
            row = pl.multiple_of(lax.rem(it, BLOCKS) * 8, 8)
            group = pl.ds(b * 3, 3)
            acc = [None] * LAYERS

            def close(l):
                v = V[group, l, pl.ds(row, 8), :] + acc[l]
                V[group, l, pl.ds(row, 8), :] = v
                U[group, l, pl.ds(row, 8), :] = U[group, l, pl.ds(row, 8), :] + time_step * v

            for l in range(LAYERS):
                for dx in (-1, 0, 1):
                    for dy in (-1, 0, 1):
                        u = L[dy + 1, group, l, pl.ds(row + MAIN + dx, 8), :]
                        for dl in (-1, 0, 1):
                            target = l - dl
                            if not 0 <= target < LAYERS:
                                continue
                            c = C[it, target, (dl + 1) * 9 + (dx + 1) * 3 + dy + 1]
                            term = c[None] * u
                            acc[target] = term if acc[target] is None else acc[target] + term
                if l > 0:
                    close(l - 1)
            close(LAYERS - 1)
            return carry

        lax.fori_loop(0, 2 * BLOCKS, one, 0)

    def contact(step):
        def fetch(i, carry):
            for k in range(8):
                p = i * 8 + k
                ROWS[pl.ds(p, 1), :] = FACES[step, pl.ds(flat_s[p], 1), :]
            return carry

        lax.fori_loop(0, PAIRS // 8, fetch, 0)
        offsets = OFFS[...]
        shifted = cyclic_shift(ROWS[...], offsets, -1)
        projected = shifted + jnp.dot(
            shifted, mortar[...], precision=lax.Precision.HIGHEST, preferred_element_type=f32
        )
        slave = SL[...]
        gap = jnp.concatenate([slave, slave], axis=0) - projected
        traction = ACT[...] * jnp.maximum(0.0, -gap)
        SF[...] = traction[:TILE] + traction[TILE:]
        back = traction + lax.dot_general(
            traction, mortar[...], (((1,), (1,)), ((), ())),
            precision=lax.Precision.HIGHEST, preferred_element_type=f32,
        )
        part = cyclic_shift(back, offsets, 1)
        coarse = part.astype(jnp.bfloat16)
        fine = (part - coarse.astype(f32)).astype(jnp.bfloat16)
        return jnp.concatenate([coarse, fine], axis=1)

    def owner_sum(part, o):
        both = jnp.dot(OH[block_of(o), :], part, preferred_element_type=f32)
        return both[:, :TILE] + both[:, TILE:]

    def send_forces(step, part):
        sends = []
        for q in range(chips):
            o = 2 * lax.rem(chip + q, chips) + 1 - core
            T[block_of(o), :] = owner_sum(part, o)
            copy = remote(
                T.at[block_of(o)], RP.at[step, q], core_send.at[step, q], core_recv.at[step, q],
                at(gx, partner),
            )
            copy.start()
            sends.append(copy)
        for q in range(chips):
            o = mate(q)
            T[block_of(o), :] = owner_sum(part, o)
        return sends

    def forward_forces(step, sends):
        out = []
        for q in list(range(1, chips)) + [0]:
            o = mate(q)
            sends[q].wait_recv()
            T[block_of(o), :] = T[block_of(o), :] + RP[step, q]
            if q > 0:
                copy = remote(
                    T.at[block_of(o)], RR.at[step, q], sum_send.at[step, q], sum_recv.at[step, q],
                    at(gx, o),
                )
                copy.start()
                out.append(copy)
        return out

    def collect_forces(step, sends, out):
        for copy in out:
            copy.wait_recv()
        force = T[block_of(gy), :]
        for q in range(1, chips):
            force = force + RR[step, q]
        return force

    def push(group, force):
        v = V[group, 0] + force
        V[group, 0] = v
        U[group, 0] = U[group, 0] + time_step * force

    copies, own = send_faces(0, disp.at[MASTER, 0])
    loads[0].wait()
    loads[1].wait()
    pack(8)
    halos = halo_copies(0, 8)
    for copy in halos:
        copy.start()

    OFFS[...] = jnp.broadcast_to(pair_v[1:2, :], (TILE, PAIRS)).T
    ACT[...] = penalty_stiffness * jnp.broadcast_to(pair_v[2:3, :], (TILE, PAIRS)).T.astype(f32)

    def hot(i, carry):
        rows = pl.ds(pl.multiple_of(i * TILE, TILE), TILE)
        index = lax.broadcasted_iota(jnp.int32, (TILE, PAIRS), 0) + i * TILE
        OH[rows, :] = jnp.where(pair_v[0:1, :] == index, 1.0, 0.0).astype(jnp.bfloat16)
        return carry

    lax.fori_loop(0, n_gy, hot, 0)
    SL[...] = clear[...] + U[SLAVE, 0]
    loads[2].wait()
    DINV[...] = time_step / D[:, 0]

    for copy in halos:
        copy.wait_recv()
    spread(0, 0, 8)
    couplings()
    finish_faces(0, copies, own)
    part = contact(0)
    sends = send_forces(0, part)
    out = forward_forces(0, sends)
    loads[3].wait()
    advance()
    push(SLAVE, DINV[1] * SF[...])
    force = collect_forces(0, sends, out)
    push(MASTER, -DINV[0] * force)

    copies, own = send_faces(1, U.at[MASTER, 0])
    for copy in halos:
        copy.wait_send()
    pack(GROUPS)
    halos = halo_copies(1, GROUPS)
    for copy in halos:
        copy.start()
    SL[...] = clear[...] + U[SLAVE, 0]
    for copy in sends + out:
        copy.wait_send()
    for copy in halos:
        copy.wait_recv()
    spread(1, 0, GROUPS)
    finish_faces(1, copies, own)
    part = contact(1)
    sends = send_forces(1, part)
    out = forward_forces(1, sends)
    advance()
    push(SLAVE, DINV[1] * SF[...])

    def store(k, block):
        return [
            pltpu.make_async_copy(ref.at[block], res.at[block], store_sem.at[which, k])
            for which, (ref, res) in enumerate(((U, u_out), (V, v_out)))
        ]

    stores = store(0, (pl.ds(0, GROUPS), pl.ds(1, LAYERS - 1)))
    stores += store(1, (pl.ds(0, 2), 0)) + store(2, (pl.ds(3, 3), 0))
    for copy in stores:
        copy.start()
    force = collect_forces(1, sends, out)
    push(MASTER, -DINV[0] * force)
    last = store(3, (MASTER, 0))
    for copy in last:
        copy.start()
    for copy in sends + out + halos:
        copy.wait_send()
    for copy in stores + last:
        copy.wait()


def body(
    n_gx, n_gy, displacement, velocity, modulus, density, clearance, mortar_coupling,
    pair_owner, pair_row, pair_offset, pair_active,
):
    owners = pair_owner.reshape(TILE, 2)
    flat = owners * TILE + pair_row.reshape(TILE, 2)
    pairs = jnp.stack([flat, pair_offset.reshape(TILE, 2), pair_active.reshape(TILE, 2)])
    pairs = pairs.transpose(0, 2, 1).reshape(3, PAIRS)
    whole = (GROUPS, LAYERS, TILE, TILE)
    hbm = pl.BlockSpec(memory_space=pl.ANY)
    vmem = pl.BlockSpec(memory_space=pltpu.VMEM)
    smem = pl.BlockSpec(memory_space=pltpu.SMEM)
    chips = n_gy // 2
    dma = pltpu.SemaphoreType.DMA
    new_disp, new_vel = pl.pallas_call(
        functools.partial(kernel, n_gx, n_gy),
        out_shape=[jax.ShapeDtypeStruct(whole, f32)] * 2,
        in_specs=[hbm, hbm, hbm, hbm, vmem, vmem, smem, vmem],
        out_specs=[hbm, hbm],
        scratch_shapes=[
            pltpu.VMEM((8, LAYERS, TILE, TILE), f32),
            pltpu.VMEM(whole, f32),
            pltpu.VMEM((2, LAYERS, TILE, TILE), f32),
            pltpu.VMEM((3, 8, LAYERS, TILE + 16, TILE), f32),
            pltpu.VMEM((2 * BLOCKS, LAYERS, 27, 8, TILE), f32),
            pltpu.VMEM((STEPS, n_gy * TILE, TILE), f32),
            pltpu.VMEM((n_gy * TILE, TILE), f32),
            pltpu.VMEM((STEPS, chips, TILE, TILE), f32),
            pltpu.VMEM((STEPS, chips, TILE, TILE), f32),
            pltpu.VMEM((n_gy * TILE, PAIRS), jnp.bfloat16),
            pltpu.VMEM((2, 64, TILE), f32),
            pltpu.VMEM((2, 64, TILE), f32),
            pltpu.VMEM((STEPS, 2, 64, TILE), f32),
            pltpu.VMEM((STEPS, 2, 64, TILE), f32),
            pltpu.VMEM((STEPS, 4, 64, TILE), f32),
            pltpu.VMEM((PAIRS, TILE), jnp.int32),
            pltpu.VMEM((PAIRS, TILE), f32),
            pltpu.VMEM((TILE, TILE), f32),
            pltpu.VMEM((TILE, TILE), f32),
            pltpu.VMEM((PAIRS, TILE), f32),
            pltpu.VMEM((2, TILE, TILE), f32),
            dma((4,)),
            dma((STEPS,)),
            dma((STEPS, 8)), dma((STEPS, 8)),
            dma((STEPS, chips)), dma((STEPS, chips)),
            dma((STEPS, chips)), dma((STEPS, chips)),
            dma((STEPS, chips)), dma((STEPS, chips)),
            dma((STEPS, chips)), dma((STEPS, chips)),
            dma((2, 4)),
        ],
        compiler_params=pltpu.CompilerParams(
            collective_id=0, has_side_effects=True, vmem_limit_bytes=62 * 1024 * 1024
        ),
        name="impact",
    )(
        displacement.reshape(whole), velocity.reshape(whole), modulus, density,
        clearance, mortar_coupling, pairs[0], pairs,
    )
    shape = displacement.shape
    return new_disp.reshape(shape), new_vel.reshape(shape)


def solution(mesh):
    n_gx, n_gy = mesh.shape["gx"], mesh.shape["gy"]
    nodes = P(None, None, None, "gx", "gy")
    pairs = P("gx", "gy", None)
    return jax.shard_map(
        functools.partial(body, n_gx, n_gy),
        mesh=mesh,
        in_specs=(
            nodes, nodes, P(None, None, "gx", "gy"), P(None, None, "gx", "gy"), P("gx", "gy"), P(),
            pairs, pairs, pairs, pairs,
        ),
        out_specs=(nodes, nodes),
        check_vma=False,
    )
```

```python
import functools

import jax
import jax.numpy as jnp
from jax import lax
from jax.experimental import pallas as pl
from jax.experimental.pallas import tpu as pltpu
from jax.sharding import PartitionSpec as P

STEPS = 2
LAYERS = 8
TILE = 128
BLOCKS = TILE // 8
PAIRS = 256
GROUPS = 6
MASTER, SLAVE = 2, 5
LOW, MAIN, HIGH = 7, 8, 136

time_step = 0.2
penalty_stiffness = 4.0

MESH = pl.DeviceIdType.MESH
f32 = jnp.float32


def lanes(shape):
    return lax.broadcasted_iota(jnp.int32, shape, len(shape) - 1)


def cyclic_shift(values, offsets, direction):
    for bit in range(7):
        amount = 1 << bit
        rolled = pltpu.roll(values, (direction * amount) % TILE, axis=1)
        values = jnp.where((offsets & amount) != 0, rolled, values)
    return values


def kernel(
    n_gx, n_gy,
    disp, vel, mod, dens, clear, mortar, owner_s, row_s, owner_v, row_v, offset_v, active_v,
    u_out, v_out,
    U, V, D, L, C, FACES, T, RP, RR, OH, XS, YS, HX, HY, HD, OFFS, ACT, SL, SF, ROWS, TR, DINV,
    load_sem, own_sem, halo_send, halo_recv, face_send, face_recv, pass_send, pass_recv,
    core_send, core_recv, sum_send, sum_recv, store_sem,
):
    gx = lax.axis_index("gx")
    gy = lax.axis_index("gy")
    core = lax.rem(gy, 2)
    chip = gy // 2
    chips = n_gy // 2
    partner = gy + 1 - 2 * core
    up = lax.rem(gx + n_gx - 1, n_gx)
    down = lax.rem(gx + 1, n_gx)
    left = lax.rem(gy + n_gy - 1, n_gy)
    right = lax.rem(gy + 1, n_gy)
    other = lax.rem(gy + n_gy - 1 + 2 * core, n_gy)

    def at(x, y):
        return {"gx": x, "gy": y}

    def mate(q):
        return 2 * lax.rem(chip + q, chips) + core

    loads = [
        pltpu.make_async_copy(disp, U.at[pl.ds(0, GROUPS)], load_sem.at[0]),
        pltpu.make_async_copy(mod, U.at[pl.ds(GROUPS, 2)], load_sem.at[1]),
        pltpu.make_async_copy(dens, D, load_sem.at[2]),
        pltpu.make_async_copy(vel, V, load_sem.at[3]),
    ]
    for load in loads:
        load.start()

    barrier = pltpu.get_barrier_semaphore()
    friends = [at(gx, mate(q)) for q in range(1, chips)]
    friends += [at(gx, partner), at(gx, other)]
    friends += [at(x, y) for x in (up, down) for y in (left, gy, right)]
    for friend in friends:
        pl.semaphore_signal(barrier, inc=1, device_id=friend, device_id_type=MESH)
    pl.semaphore_wait(barrier, len(friends))

    def remote(src, dst, send, recv, target):
        return pltpu.make_async_remote_copy(
            src_ref=src, dst_ref=dst, send_sem=send, recv_sem=recv,
            device_id=target, device_id_type=MESH,
        )

    def block_of(j):
        return pl.ds(pl.multiple_of(j * TILE, TILE), TILE)

    def face_copies(step, src):
        mine = FACES.at[step, block_of(gy)]
        out = [remote(src, mine, face_send.at[step, 0], face_recv.at[step, 0], at(gx, partner))]
        for q in range(1, chips):
            out.append(remote(src, mine, face_send.at[step, q], face_recv.at[step, q], at(gx, mate(q))))
        return out

    def pass_copy(step, q):
        held = FACES.at[step, block_of(mate(chips - q))]
        return remote(held, held, pass_send.at[step, q], pass_recv.at[step, q], at(gx, partner))

    def send_faces(step, src):
        copies = face_copies(step, src)
        for q in near + [0]:
            copies[q].start()
        own = pltpu.make_async_copy(src, FACES.at[step, block_of(gy)], own_sem.at[step])
        own.start()
        return copies, own

    near = [1, chips - 1] + list(range(2, chips - 1))

    def pass_faces(step, copies, order):
        passed = []
        for q in order:
            copies[q].wait_recv()
            copy = pass_copy(step, q)
            copy.start()
            passed.append(copy)
        return passed

    def finish_faces(copies, own, passed):
        own.wait()
        copies[0].wait_recv()
        for copy in passed:
            copy.wait_recv()
        for copy in copies + passed:
            copy.wait_send()

    def pack(first, groups):
        def one(i, carry):
            g = i // 2
            half = lax.rem(i, 2)
            lane = lanes((8, TILE)) // 2
            packed = jnp.zeros((8, TILE), f32)
            for t in range(4 * BLOCKS):
                tile = U[g, half * 4 + t // BLOCKS, t % BLOCKS * 8 : t % BLOCKS * 8 + 8, :]
                packed = jnp.where(lane == t, pltpu.roll(tile, 2 * t + 1, axis=1), packed)
            YS[pl.ds(pl.multiple_of(i * 8, 8), 8), :] = packed
            for k in range(4):
                l = half * 4 + k
                XS[0, pl.ds(g * 8 + l, 1), :] = U[g, l, 0:1, :]
                XS[1, pl.ds(g * 8 + l, 1), :] = U[g, l, TILE - 1 : TILE, :]
            return carry

        lax.fori_loop(2 * first, 2 * (first + groups), one, 0)

    def halo_copies(phase, step, first, groups):
        rows = pl.ds(first * 8, groups * 8)
        wide = pl.ds(first * 16, groups * 16)
        plan = [
            (XS.at[0, rows], HX.at[step, 1, rows], at(up, gy)),
            (XS.at[1, rows], HX.at[step, 0, rows], at(down, gy)),
            (YS.at[wide], HY.at[step, 1, wide], at(gx, left)),
            (YS.at[wide], HY.at[step, 0, wide], at(gx, right)),
            (XS.at[0, rows], HD.at[step, 3, rows], at(up, left)),
            (XS.at[0, rows], HD.at[step, 2, rows], at(up, right)),
            (XS.at[1, rows], HD.at[step, 1, rows], at(down, left)),
            (XS.at[1, rows], HD.at[step, 0, rows], at(down, right)),
        ]
        return [
            remote(src, dst, halo_send.at[phase, k], halo_recv.at[phase, k], target)
            for k, (src, dst, target) in enumerate(plan)
        ]

    def send_halos(phase, step, first, groups):
        pack(first, groups)
        copies = halo_copies(phase, step, first, groups)
        for copy in copies:
            copy.start()
        return copies

    def spread(step, first, groups):
        at_top = (gx == 0).astype(f32)
        at_bottom = (gx == n_gx - 1).astype(f32)
        at_left = (gy == 0).astype(f32)
        at_right = (gy == n_gy - 1).astype(f32)

        def one(g, carry):
            is_mod = (g >= GROUPS).astype(f32)
            keep_top, keep_bottom = 1.0 - is_mod * at_top, 1.0 - is_mod * at_bottom
            keep_left, keep_right = 1.0 - is_mod * at_left, 1.0 - is_mod * at_right
            lane = lanes((8, TILE))
            rows = pl.ds(pl.multiple_of(g * 8, 8), 8)

            def part(half, carry):
                wide = pl.ds(pl.multiple_of(g * 16 + half * 8, 8), 8)
                low = HY[step, 0, wide, :] * keep_left
                high = HY[step, 1, wide, :] * keep_right
                even = lane % 2 == 0
                both = jnp.where(even, pltpu.roll(high, TILE - 1, axis=1), pltpu.roll(low, 1, axis=1))
                for t in range(4 * BLOCKS):
                    l = half * 4 + t // BLOCKS
                    row = t % BLOCKS * 8
                    edge = pltpu.roll(both, TILE - 1 - 2 * t, axis=1)
                    here = U[g, l, row : row + 8, :]
                    into = slice(MAIN + row, MAIN + row + 8)
                    L[0, g, l, into, :] = jnp.where(lane == 0, edge, pltpu.roll(here, 1, axis=1))
                    L[1, g, l, into, :] = here
                    L[2, g, l, into, :] = jnp.where(lane == TILE - 1, edge, pltpu.roll(here, TILE - 1, axis=1))
                return carry

            lax.fori_loop(0, 2, part, 0)
            for side, keep, spot in ((0, keep_top, LOW), (1, keep_bottom, HIGH)):
                here = HX[step, side, rows, :] * keep
                corner_low = HD[step, 2 * side, rows, :] * (keep * keep_left)
                corner_high = HD[step, 2 * side + 1, rows, :] * (keep * keep_right)
                before = pltpu.roll(jnp.where(lane == TILE - 1, corner_low, here), 1, axis=1)
                after = pltpu.roll(jnp.where(lane == 0, corner_high, here), TILE - 1, axis=1)
                for dy, plane in enumerate((before, here, after)):
                    for l in range(LAYERS):
                        L[dy, g, l, spot : spot + 1, :] = plane[l : l + 1, :]
            return carry

        lax.fori_loop(first, first + groups, one, 0)

    def couplings(first, last):
        def one(it, carry):
            b = it // (BLOCKS // 2 * LAYERS)
            t = lax.rem(it // LAYERS, BLOCKS // 2)
            l = lax.rem(it, LAYERS)
            row = pl.multiple_of(t * 16, 16)
            own = L[1, GROUPS + b, l, pl.ds(row + MAIN, 16), :]
            base = own * ((2.0 * time_step) / D[b, l, pl.ds(row, 16), :])
            total = jnp.zeros((16, TILE), f32)
            for dl in (-1, 0, 1):
                near = jnp.clip(l + dl, 0, LAYERS - 1)
                inside = jnp.logical_and(l + dl >= 0, l + dl < LAYERS).astype(f32)
                scaled = base if dl == 0 else base * inside
                weights = [scaled, scaled * 0.5, scaled * 0.25] if dl else [None, scaled, scaled * 0.5]
                for dx in (-1, 0, 1):
                    for dy in (-1, 0, 1):
                        if dl == dx == dy == 0:
                            continue
                        e = L[dy + 1, GROUPS + b, near, pl.ds(row + MAIN + dx, 16), :]
                        c = weights[abs(dx) + abs(dy)] * (e * pl.reciprocal(own + e, approx=True))
                        C[b * (BLOCKS // 2) + t, l, (dl + 1) * 9 + (dx + 1) * 3 + dy + 1] = c
                        total = total + c
            C[b * (BLOCKS // 2) + t, l, 13] = -total
            return carry

        lax.fori_loop(first, last, one, 0)

    def advance(first, last):
        def one(it, carry):
            b = it // BLOCKS
            row = pl.multiple_of(lax.rem(it, BLOCKS) * 8, 8)
            odd = pl.multiple_of(lax.rem(it, 2) * 8, 8)
            group = pl.ds(b * 3, 3)
            acc = [None] * LAYERS

            def close(l):
                v = V[group, l, pl.ds(row, 8), :] + acc[l]
                V[group, l, pl.ds(row, 8), :] = v
                U[group, l, pl.ds(row, 8), :] = U[group, l, pl.ds(row, 8), :] + time_step * v

            for l in range(LAYERS):
                for dx in (-1, 0, 1):
                    for dy in (-1, 0, 1):
                        u = L[dy + 1, group, l, pl.ds(row + MAIN + dx, 8), :]
                        for dl in (-1, 0, 1):
                            target = l - dl
                            if not 0 <= target < LAYERS:
                                continue
                            c = C[it // 2, target, (dl + 1) * 9 + (dx + 1) * 3 + dy + 1, pl.ds(odd, 8)]
                            term = c[None] * u
                            acc[target] = term if acc[target] is None else acc[target] + term
                if l > 0:
                    close(l - 1)
            close(LAYERS - 1)
            return carry

        lax.fori_loop(first, last, one, 0)

    def contact(step):
        def fetch(i, carry):
            for k in range(8):
                p = i * 8 + k
                ROWS[pl.ds(p, 1), :] = FACES[step, pl.ds(owner_s[0, 0, p] * TILE + row_s[0, 0, p], 1), :]
            return carry

        lax.fori_loop(0, PAIRS // 8, fetch, 0)
        offsets = OFFS[...]
        shifted = cyclic_shift(ROWS[...], offsets, -1)
        projected = shifted + jnp.dot(
            shifted, mortar[...], precision=lax.Precision.HIGHEST, preferred_element_type=f32
        )
        traction = ACT[...] * jnp.maximum(0.0, projected - SL[...])
        TR[...] = traction
        SF[...] = TR[pl.ds(0, TILE, stride=2), :] + TR[pl.ds(1, TILE, stride=2), :]
        back = traction + lax.dot_general(
            traction, mortar[...], (((1,), (1,)), ((), ())),
            precision=lax.Precision.HIGHEST, preferred_element_type=f32,
        )
        part = cyclic_shift(back, offsets, 1)
        coarse = part.astype(jnp.bfloat16)
        fine = (part - coarse.astype(f32)).astype(jnp.bfloat16)
        return jnp.concatenate([coarse, fine], axis=1)

    def owner_sum(part, o):
        both = jnp.dot(OH[block_of(o), :], part, preferred_element_type=f32)
        return both[:, :TILE] + both[:, TILE:]

    def send_forces(step, part):
        sends = [None] * chips
        for q in near + [0]:
            o = 2 * lax.rem(chip + q, chips) + 1 - core
            T[block_of(o), :] = owner_sum(part, o)
            copy = remote(
                T.at[block_of(o)], RP.at[step, q], core_send.at[step, q], core_recv.at[step, q],
                at(gx, partner),
            )
            copy.start()
            sends[q] = copy
        for q in range(chips):
            o = mate(q)
            T[block_of(o), :] = owner_sum(part, o)
        return sends

    def forward_forces(step, sends, order):
        out = []
        for q in order:
            o = mate(q)
            sends[q].wait_recv()
            T[block_of(o), :] = T[block_of(o), :] + RP[step, q]
            if q > 0:
                copy = remote(
                    T.at[block_of(o)], RR.at[step, q], sum_send.at[step, q], sum_recv.at[step, q],
                    at(gx, o),
                )
                copy.start()
                out.append(copy)
        return out

    def collect_forces(step, out):
        for copy in out:
            copy.wait_recv()
        force = T[block_of(gy), :]
        for q in range(1, chips):
            force = force + RR[step, q]
        return force

    def push(group, force):
        v = V[group, 0] + force
        V[group, 0] = v
        U[group, 0] = U[group, 0] + time_step * force

    copies, own = send_faces(0, disp.at[MASTER, 0])
    loads[0].wait()
    loads[1].wait()
    halos = send_halos(0, 0, 0, 8)

    OFFS[...] = jnp.broadcast_to(offset_v[0], (TILE, PAIRS)).T
    ACT[...] = penalty_stiffness * jnp.broadcast_to(active_v[0], (TILE, PAIRS)).T.astype(f32)

    def hot(i, carry):
        rows = pl.ds(pl.multiple_of(i * TILE, TILE), TILE)
        index = lax.broadcasted_iota(jnp.int32, (TILE, PAIRS), 0) + i * TILE
        OH[rows, :] = jnp.where(owner_v[0] * TILE + row_v[0] == index, 1.0, 0.0).astype(jnp.bfloat16)
        return carry

    lax.fori_loop(0, n_gy, hot, 0)

    def slave_gaps():
        rest = clear[...] + U[SLAVE, 0]
        SL[pl.ds(0, TILE, stride=2), :] = rest
        SL[pl.ds(1, TILE, stride=2), :] = rest

    slave_gaps()
    for copy in halos:
        copy.wait_recv()
    spread(0, GROUPS, 2)
    passed = pass_faces(0, copies, near)
    spread(0, 0, GROUPS)
    finish_faces(copies, own, passed)
    part = contact(0)
    sends = send_forces(0, part)
    loads[2].wait()
    DINV[...] = time_step / D[:, 0]
    half = BLOCKS * LAYERS // 2
    couplings(0, half)
    out = forward_forces(0, sends, near + [0])
    couplings(half, 2 * half)
    loads[3].wait()
    advance(BLOCKS, 2 * BLOCKS)
    push(SLAVE, DINV[1] * SF[...])
    for copy in halos:
        copy.wait_send()
    halos = send_halos(1, 1, 3, 3)
    slave_gaps()
    advance(0, BLOCKS)
    force = collect_forces(0, out)
    push(MASTER, -DINV[0] * force)

    copies, own = send_faces(1, U.at[MASTER, 0])
    more = send_halos(2, 1, 0, 3)
    for copy in sends + out:
        copy.wait_send()
    for copy in halos:
        copy.wait_recv()
    spread(1, 3, 3)
    for copy in more:
        copy.wait_recv()
    spread(1, 0, 3)
    passed = pass_faces(1, copies, near)
    finish_faces(copies, own, passed)
    part = contact(1)
    sends = send_forces(1, part)
    advance(0, 4)
    out = []
    for k, q in enumerate(near):
        advance(4 + 2 * k, 6 + 2 * k)
        out += forward_forces(1, sends, [q])
    forward_forces(1, sends, [0])
    advance(2 + 2 * chips, 2 * BLOCKS)
    push(SLAVE, DINV[1] * SF[...])

    def store(k, block):
        return [
            pltpu.make_async_copy(ref.at[block], res.at[block], store_sem.at[which, k])
            for which, (ref, res) in enumerate(((U, u_out), (V, v_out)))
        ]

    stores = store(0, (pl.ds(0, GROUPS), pl.ds(1, LAYERS - 1)))
    stores += store(1, (pl.ds(0, 2), 0)) + store(2, (pl.ds(3, 3), 0))
    for copy in stores:
        copy.start()
    force = collect_forces(1, out)
    push(MASTER, -DINV[0] * force)
    last = store(3, (MASTER, 0))
    for copy in last:
        copy.start()
    for copy in sends + out + halos + more:
        copy.wait_send()
    for copy in stores + last:
        copy.wait()


def body(
    n_gx, n_gy, displacement, velocity, modulus, density, clearance, mortar_coupling,
    pair_owner, pair_row, pair_offset, pair_active,
):
    owner, row, offset, active = (
        x.transpose(0, 2, 1) for x in (pair_owner, pair_row, pair_offset, pair_active)
    )
    whole = (GROUPS, LAYERS, TILE, TILE)
    hbm = pl.BlockSpec(memory_space=pl.ANY)
    vmem = pl.BlockSpec(memory_space=pltpu.VMEM)
    smem = pl.BlockSpec(memory_space=pltpu.SMEM)
    chips = n_gy // 2
    dma = pltpu.SemaphoreType.DMA
    new_disp, new_vel = pl.pallas_call(
        functools.partial(kernel, n_gx, n_gy),
        out_shape=[jax.ShapeDtypeStruct(whole, f32)] * 2,
        in_specs=[hbm] * 4 + [vmem] * 2 + [smem] * 2 + [vmem] * 4,
        out_specs=[hbm, hbm],
        scratch_shapes=[
            pltpu.VMEM((8, LAYERS, TILE, TILE), f32),
            pltpu.VMEM(whole, f32),
            pltpu.VMEM((2, LAYERS, TILE, TILE), f32),
            pltpu.VMEM((3, 8, LAYERS, TILE + 16, TILE), f32),
            pltpu.VMEM((BLOCKS, LAYERS, 27, 16, TILE), f32),
            pltpu.VMEM((STEPS, n_gy * TILE, TILE), f32),
            pltpu.VMEM((n_gy * TILE, TILE), f32),
            pltpu.VMEM((STEPS, chips, TILE, TILE), f32),
            pltpu.VMEM((STEPS, chips, TILE, TILE), f32),
            pltpu.VMEM((n_gy * TILE, PAIRS), jnp.bfloat16),
            pltpu.VMEM((2, 64, TILE), f32),
            pltpu.VMEM((128, TILE), f32),
            pltpu.VMEM((STEPS, 2, 64, TILE), f32),
            pltpu.VMEM((STEPS, 2, 128, TILE), f32),
            pltpu.VMEM((STEPS, 4, 64, TILE), f32),
            pltpu.VMEM((PAIRS, TILE), jnp.int32),
            pltpu.VMEM((PAIRS, TILE), f32),
            pltpu.VMEM((PAIRS, TILE), f32),
            pltpu.VMEM((TILE, TILE), f32),
            pltpu.VMEM((PAIRS, TILE), f32),
            pltpu.VMEM((PAIRS, TILE), f32),
            pltpu.VMEM((2, TILE, TILE), f32),
            dma((4,)),
            dma((STEPS,)),
            dma((3, 8)), dma((3, 8)),
            dma((STEPS, chips)), dma((STEPS, chips)),
            dma((STEPS, chips)), dma((STEPS, chips)),
            dma((STEPS, chips)), dma((STEPS, chips)),
            dma((STEPS, chips)), dma((STEPS, chips)),
            dma((2, 4)),
        ],
        compiler_params=pltpu.CompilerParams(
            collective_id=0, has_side_effects=True, vmem_limit_bytes=62 * 1024 * 1024
        ),
        name="impact",
    )(
        displacement.reshape(whole), velocity.reshape(whole), modulus, density,
        clearance, mortar_coupling, owner, row, owner, row, offset, active,
    )
    shape = displacement.shape
    return new_disp.reshape(shape), new_vel.reshape(shape)


def solution(mesh):
    n_gx, n_gy = mesh.shape["gx"], mesh.shape["gy"]
    nodes = P(None, None, None, "gx", "gy")
    pairs = P("gx", "gy", None)
    return jax.shard_map(
        functools.partial(body, n_gx, n_gy),
        mesh=mesh,
        in_specs=(
            nodes, nodes, P(None, None, "gx", "gy"), P(None, None, "gx", "gy"), P("gx", "gy"), P(),
            pairs, pairs, pairs, pairs,
        ),
        out_specs=(nodes, nodes),
        check_vma=False,
    )
```

```python
import functools

import jax
import jax.numpy as jnp
from jax import lax
from jax.experimental import pallas as pl
from jax.experimental.pallas import tpu as pltpu
from jax.sharding import PartitionSpec as P

STEPS = 2
LAYERS = 8
TILE = 128
BLOCKS = TILE // 8
PAIRS = 256
GROUPS = 6
MASTER, SLAVE = 2, 5
LOW, MAIN, HIGH = 7, 8, 136

time_step = 0.2
penalty_stiffness = 4.0

VMEM_LIMIT = 62 * 1024 * 1024

MESH = pl.DeviceIdType.MESH
f32 = jnp.float32


def lanes(shape):
    return lax.broadcasted_iota(jnp.int32, shape, len(shape) - 1)


def cyclic_shift(values, offsets, direction):
    for bit in range(7):
        amount = 1 << bit
        rolled = pltpu.roll(values, (direction * amount) % TILE, axis=1)
        values = jnp.where((offsets & amount) != 0, rolled, values)
    return values


def kernel(
    n_gx, n_gy,
    disp, vel, mod, dens, clear, mortar, owner_s, row_s, owner_v, row_v, offset_v, active_v,
    u_out, v_out,
    U, V, E, D, L, C, FACES, T, PART, RR, OH, FLAT, XS, YS, CS, HX, HY, HD, OFFS, ACT, SL, SF, ROWS, TR, DINV,
    load_sem, own_sem, halo_send, halo_recv, face_send, face_recv, pass_send, pass_recv,
    core_send, core_recv, sum_send, sum_recv, store_sem,
):
    gx = lax.axis_index("gx")
    gy = lax.axis_index("gy")
    core = lax.rem(gy, 2)
    plane = n_gy // 2
    ring = n_gy // 4
    partner = gy + 1 - 2 * core
    up = lax.rem(gx + n_gx - 1, n_gx)
    down = lax.rem(gx + 1, n_gx)
    left = lax.rem(gy + n_gy - 1, n_gy)
    right = lax.rem(gy + 1, n_gy)
    other = lax.rem(gy + n_gy - 1 + 2 * core, n_gy)

    def at(x, y):
        return {"gx": x, "gy": y}

    def mate(dz, dy):
        z = lax.rem(gy // plane + dz, 2)
        y = lax.rem(lax.rem(gy, plane) // 2 + dy, ring)
        return z * plane + 2 * y + core

    loads = [
        pltpu.make_async_copy(disp, U, load_sem.at[0]),
        pltpu.make_async_copy(mod, E, load_sem.at[1]),
        pltpu.make_async_copy(dens, D, load_sem.at[2]),
        pltpu.make_async_copy(vel, V, load_sem.at[3]),
    ]
    for load in loads:
        load.start()

    barrier = pltpu.get_barrier_semaphore()
    friends = [at(gx, mate(*d)) for d in ((0, 1), (0, 2), (0, 3), (1, 0))]
    friends += [at(gx, partner), at(gx, other)]
    friends += [at(x, y) for x in (up, down) for y in (left, gy, right)]
    for friend in friends:
        pl.semaphore_signal(barrier, inc=1, device_id=friend, device_id_type=MESH)
    pl.semaphore_wait(barrier, len(friends))

    def remote(src, dst, send, recv, target):
        return pltpu.make_async_remote_copy(
            src_ref=src, dst_ref=dst, send_sem=send, recv_sem=recv,
            device_id=target, device_id_type=MESH,
        )

    def block_of(j):
        return pl.ds(pl.multiple_of(j * TILE, TILE), TILE)

    def relay(step, dz, dy, k, target):
        held = FACES.at[step, block_of(mate(dz, dy))]
        return remote(held, held, face_send.at[step, k], face_recv.at[step, k], at(gx, target))

    def send_faces(step, src):
        mine = FACES.at[step, block_of(gy)]
        copies = {}
        for k, target in ((4, mate(1, 0)), (2, mate(0, 2)), (1, mate(0, 3)), (3, mate(0, 1)), (0, partner)):
            copies[k] = remote(src, mine, face_send.at[step, k], face_recv.at[step, k], at(gx, target))
            copies[k].start()
        own = pltpu.make_async_copy(src, mine, own_sem.at[step])
        own.start()
        return copies, own

    def share(step, copies, k):
        copies[k].wait_recv()
        held = FACES.at[step, block_of(mate(k // 4, k % 4))]
        copies[8 + k] = remote(held, held, pass_send.at[step, k], pass_recv.at[step, k], at(gx, partner))
        copies[8 + k].start()

    def relay_faces(step, copies):
        share(step, copies, 4)
        copies[5] = relay(step, 1, 0, 5, mate(0, 3))
        copies[7] = relay(step, 1, 0, 7, mate(0, 1))
        copies[5].start()
        copies[7].start()
        share(step, copies, 2)
        copies[6] = relay(step, 0, 2, 6, mate(1, 0))
        copies[6].start()

    def finish_faces(step, copies, own):
        for k in (1, 3, 5, 7, 6):
            share(step, copies, k)
        own.wait()
        copies[0].wait_recv()
        for k in range(1, 8):
            copies[8 + k].wait_recv()
        for k in copies:
            copies[k].wait_send()

    def pack(phase, src, base, first, groups):
        def one(g, carry):
            lane = lanes((8, TILE))
            halves = []
            for half in range(2):
                packed = jnp.zeros((8, TILE), f32)
                for t in range(4 * BLOCKS):
                    tile = src[g - base, half * 4 + t // BLOCKS, t % BLOCKS * 8 : t % BLOCKS * 8 + 8, :]
                    packed = jnp.where(lane // 2 == t, pltpu.roll(tile, 2 * t + 1, axis=1), packed)
                halves.append(packed)
            even = lane % 2 == 0
            to_right = jnp.where(even, halves[0], pltpu.roll(halves[1], 1, axis=1))
            to_left = jnp.where(even, pltpu.roll(halves[1], TILE - 1, axis=1), halves[0])
            rows = pl.ds(pl.multiple_of(g * 8, 8), 8)
            for side, columns in enumerate((to_left, to_right)):
                YS[side, rows, :] = columns
                CS[phase, side, pl.ds(g, 1), :] = columns[0:1, :]
                CS[phase, 2 + side, pl.ds(g, 1), :] = columns[7:8, :]
            for l in range(LAYERS):
                XS[0, pl.ds(g * 8 + l, 1), :] = src[g - base, l, 0:1, :]
                XS[1, pl.ds(g * 8 + l, 1), :] = src[g - base, l, TILE - 1 : TILE, :]
            return carry

        lax.fori_loop(first, first + groups, one, 0)

    def halo_copies(phase, first, groups):
        step = 1 if phase in (1, 2) else 0
        rows = pl.ds(first * 8, groups * 8)
        plan = [
            (XS.at[0, rows], HX.at[step, 1, rows], at(up, gy)),
            (XS.at[1, rows], HX.at[step, 0, rows], at(down, gy)),
            (YS.at[0, rows], HY.at[step, 1, rows], at(gx, left)),
            (YS.at[1, rows], HY.at[step, 0, rows], at(gx, right)),
            (CS.at[phase, 0], HD.at[phase, 3], at(up, left)),
            (CS.at[phase, 1], HD.at[phase, 2], at(up, right)),
            (CS.at[phase, 2], HD.at[phase, 1], at(down, left)),
            (CS.at[phase, 3], HD.at[phase, 0], at(down, right)),
        ]
        return [
            remote(src, dst, halo_send.at[phase, k], halo_recv.at[phase, k], target)
            for k, (src, dst, target) in enumerate(plan)
        ]

    def send_halos(phase, src, base, first, groups):
        pack(phase, src, base, first, groups)
        copies = halo_copies(phase, first, groups)
        for copy in copies:
            copy.start()
        return copies

    def spread(phase, src, base, first, groups):
        step = 1 if phase in (1, 2) else 0
        at_top = (gx == 0).astype(f32)
        at_bottom = (gx == n_gx - 1).astype(f32)
        at_left = (gy == 0).astype(f32)
        at_right = (gy == n_gy - 1).astype(f32)

        def one(g, carry):
            is_mod = (g >= GROUPS).astype(f32)
            keep_top, keep_bottom = 1.0 - is_mod * at_top, 1.0 - is_mod * at_bottom
            keep_left, keep_right = 1.0 - is_mod * at_left, 1.0 - is_mod * at_right
            lane = lanes((8, TILE))
            rows = pl.ds(pl.multiple_of(g * 8, 8), 8)

            low = HY[step, 0, rows, :] * keep_left
            high = HY[step, 1, rows, :] * keep_right
            even = lane % 2 == 0
            for half in range(2):
                if half == 0:
                    both = jnp.where(even, pltpu.roll(high, TILE - 1, axis=1), pltpu.roll(low, 1, axis=1))
                else:
                    both = jnp.where(even, high, low)
                for t in range(4 * BLOCKS):
                    l = half * 4 + t // BLOCKS
                    row = t % BLOCKS * 8
                    edge = pltpu.roll(both, TILE - 1 - 2 * t, axis=1)
                    here = src[g - base, l, row : row + 8, :]
                    into = slice(MAIN + row, MAIN + row + 8)
                    L[0, g, l, into, :] = jnp.where(lane == 0, edge, pltpu.roll(here, 1, axis=1))
                    L[1, g, l, into, :] = here
                    L[2, g, l, into, :] = jnp.where(lane == TILE - 1, edge, pltpu.roll(here, TILE - 1, axis=1))
            layer = lax.broadcasted_iota(jnp.int32, (LAYERS, TILE), 0)
            upper = layer // 4

            def corner(k, block, flip):
                spot = 32 * (layer % 4) + 2 * block + (1 - upper if flip else upper)
                row = jnp.broadcast_to(HD[phase, k, pl.ds(g, 1), :], (LAYERS, TILE))
                return jnp.sum(jnp.where(lane == spot, row, 0.0), axis=1, keepdims=True)

            for side, keep, spot in ((0, keep_top, LOW), (1, keep_bottom, HIGH)):
                here = HX[step, side, rows, :] * keep
                block = 0 if side else BLOCKS - 1
                corner_low = corner(2 * side, block, False) * (keep * keep_left)
                corner_high = corner(2 * side + 1, block, True) * (keep * keep_right)
                before = pltpu.roll(jnp.where(lane == TILE - 1, corner_low, here), 1, axis=1)
                after = pltpu.roll(jnp.where(lane == 0, corner_high, here), TILE - 1, axis=1)
                for dy, plane in enumerate((before, here, after)):
                    for l in range(LAYERS):
                        L[dy, g, l, spot : spot + 1, :] = plane[l : l + 1, :]
            return carry

        lax.fori_loop(first, first + groups, one, 0)

    def couplings(first, last):
        def one(it, carry):
            b = it // (BLOCKS // 2 * LAYERS)
            t = lax.rem(it // LAYERS, BLOCKS // 2)
            l = lax.rem(it, LAYERS)
            row = pl.multiple_of(t * 16, 16)
            own = L[1, GROUPS + b, l, pl.ds(row + MAIN, 16), :]
            base = own * ((2.0 * time_step) / D[b, l, pl.ds(row, 16), :])
            total = jnp.zeros((16, TILE), f32)
            for dl in (-1, 0, 1):
                near = jnp.clip(l + dl, 0, LAYERS - 1)
                inside = jnp.logical_and(l + dl >= 0, l + dl < LAYERS).astype(f32)
                scaled = base if dl == 0 else base * inside
                weights = [scaled, scaled * 0.5, scaled * 0.25] if dl else [None, scaled, scaled * 0.5]
                for dx in (-1, 0, 1):
                    for dy in (-1, 0, 1):
                        if dl == dx == dy == 0:
                            continue
                        e = L[dy + 1, GROUPS + b, near, pl.ds(row + MAIN + dx, 16), :]
                        c = weights[abs(dx) + abs(dy)] * (e * pl.reciprocal(own + e, approx=True))
                        C[b * (BLOCKS // 2) + t, l, (dl + 1) * 9 + (dx + 1) * 3 + dy + 1] = c
                        total = total + c
            C[b * (BLOCKS // 2) + t, l, 13] = -total
            return carry

        lax.fori_loop(first, last, one, 0)

    def advance(first, last):
        def one(it, carry):
            b = it // BLOCKS
            row = pl.multiple_of(lax.rem(it, BLOCKS) * 8, 8)
            odd = pl.multiple_of(lax.rem(it, 2) * 8, 8)
            group = pl.ds(b * 3, 3)
            acc = [None] * LAYERS

            def close(l):
                v = V[group, l, pl.ds(row, 8), :] + acc[l]
                V[group, l, pl.ds(row, 8), :] = v
                U[group, l, pl.ds(row, 8), :] = U[group, l, pl.ds(row, 8), :] + time_step * v

            for l in range(LAYERS):
                for dx in (-1, 0, 1):
                    for dy in (-1, 0, 1):
                        u = L[dy + 1, group, l, pl.ds(row + MAIN + dx, 8), :]
                        for dl in (-1, 0, 1):
                            target = l - dl
                            if not 0 <= target < LAYERS:
                                continue
                            c = C[it // 2, target, (dl + 1) * 9 + (dx + 1) * 3 + dy + 1, pl.ds(odd, 8)]
                            term = c[None] * u
                            acc[target] = term if acc[target] is None else acc[target] + term
                if l > 0:
                    close(l - 1)
            close(LAYERS - 1)
            return carry

        lax.fori_loop(first, last, one, 0)

    def contact(step):
        def fetch(i, carry):
            for k in range(8):
                p = i * 8 + k
                ROWS[pl.ds(p, 1), :] = FACES[step, pl.ds(owner_s[0, 0, p] * TILE + row_s[0, 0, p], 1), :]
            return carry

        lax.fori_loop(0, PAIRS // 8, fetch, 0)
        offsets = OFFS[...]
        shifted = cyclic_shift(ROWS[...], offsets, -1)
        projected = shifted + jnp.dot(
            shifted, mortar[...], precision=lax.Precision.HIGHEST, preferred_element_type=f32
        )
        traction = ACT[...] * jnp.maximum(0.0, projected - SL[...])
        TR[...] = traction
        SF[...] = TR[pl.ds(0, TILE, stride=2), :] + TR[pl.ds(1, TILE, stride=2), :]
        back = traction + lax.dot_general(
            traction, mortar[...], (((1,), (1,)), ((), ())),
            precision=lax.Precision.HIGHEST, preferred_element_type=f32,
        )
        PART[step, 0] = cyclic_shift(back, offsets, 1)
        copy = remote(PART.at[step, 0], PART.at[step, 1], core_send.at[step], core_recv.at[step], at(gx, partner))
        copy.start()
        return copy

    order = ((1, 1), (1, 3), (1, 2), (0, 1), (0, 3), (1, 0), (0, 2), (0, 0))

    def split(values):
        coarse = values.astype(jnp.bfloat16)
        return jnp.concatenate([coarse, (values - coarse.astype(f32)).astype(jnp.bfloat16)], axis=1)

    def rows_of(there):
        return block_of(mate(*there) // 2)

    def first_sums(step, exchange):
        exchange.wait_recv()
        part = jnp.concatenate([split(PART[step, 0]), split(PART[step, 1])], axis=0)
        targets = ((0, 1), (0, 3), (1, 0), (0, 1), (0, 3))
        out = []
        for k, there in enumerate(order):
            rows = rows_of(there)
            both = jnp.dot(OH[rows, :], part, preferred_element_type=f32)
            T[rows, :] = both[:, :TILE] + both[:, TILE:]
            if k < len(targets):
                out.append(send_sum(step, there, k, targets[k]))
        return out

    def send_sum(step, there, k, target):
        copy = remote(
            T.at[rows_of(there)], RR.at[step, k], sum_send.at[step, k], sum_recv.at[step, k],
            at(gx, mate(*target)),
        )
        copy.start()
        return copy

    def second_sums(step, out):
        out[0].wait_recv()
        out[1].wait_recv()
        rows = rows_of((1, 0))
        T[rows, :] = T[rows, :] + RR[step, 0] + RR[step, 1]
        out.append(send_sum(step, (1, 0), 5, (1, 0)))
        out[2].wait_recv()
        rows = rows_of((0, 2))
        T[rows, :] = T[rows, :] + RR[step, 2]
        out.append(send_sum(step, (0, 2), 6, (0, 2)))

    def collect_forces(step, out):
        force = T[rows_of((0, 0)), :]
        for k in (3, 4, 6, 5):
            out[k].wait_recv()
            force = force + RR[step, k]
        return force

    def push(group, force):
        v = V[group, 0] + force
        V[group, 0] = v
        U[group, 0] = U[group, 0] + time_step * force

    copies, own = send_faces(0, disp.at[MASTER, 0])
    FLAT[0] = jnp.broadcast_to(owner_v[0] * TILE + row_v[0], (8, PAIRS))
    indices = remote(FLAT.at[0], FLAT.at[1], core_send.at[2], core_recv.at[2], at(gx, partner))
    indices.start()
    loads[1].wait()
    stiff = send_halos(3, E, GROUPS, GROUPS, 2)
    loads[0].wait()
    halos = send_halos(0, U, 0, 0, GROUPS)

    OFFS[...] = jnp.broadcast_to(offset_v[0], (TILE, PAIRS)).T
    ACT[...] = penalty_stiffness * jnp.broadcast_to(active_v[0], (TILE, PAIRS)).T.astype(f32)
    indices.wait_recv()

    def hot(m, carry):
        rows = pl.ds(pl.multiple_of(m * TILE, TILE), TILE)
        index = lax.broadcasted_iota(jnp.int32, (TILE, PAIRS), 0) + (2 * m + core) * TILE
        for side in range(2):
            OH[rows, side * PAIRS : (side + 1) * PAIRS] = jnp.where(
                FLAT[side, 0:1, :] == index, 1.0, 0.0
            ).astype(jnp.bfloat16)
        return carry

    lax.fori_loop(0, n_gy // 2, hot, 0)

    def slave_gaps():
        rest = clear[...] + U[SLAVE, 0]
        SL[pl.ds(0, TILE, stride=2), :] = rest
        SL[pl.ds(1, TILE, stride=2), :] = rest

    slave_gaps()
    relay_faces(0, copies)
    for copy in stiff:
        copy.wait_recv()
    spread(3, E, GROUPS, GROUPS, 2)
    loads[2].wait()
    DINV[...] = time_step / D[:, 0]
    half = BLOCKS * LAYERS // 2
    couplings(0, half)
    finish_faces(0, copies, own)
    exchange = contact(0)
    for copy in halos:
        copy.wait_recv()
    spread(0, U, 0, 0, 3)
    out = first_sums(0, exchange)
    spread(0, U, 0, 3, 3)
    loads[3].wait()
    advance(0, BLOCKS)
    second_sums(0, out)
    couplings(half, 2 * half)
    force = collect_forces(0, out)
    push(MASTER, -DINV[0] * force)

    copies, own = send_faces(1, U.at[MASTER, 0])
    for copy in halos + stiff:
        copy.wait_send()
    halos = send_halos(1, U, 0, 0, 3)
    advance(BLOCKS, 2 * BLOCKS)
    push(SLAVE, DINV[1] * SF[...])
    more = send_halos(2, U, 0, 3, 3)
    relay_faces(1, copies)
    slave_gaps()
    for copy in out:
        copy.wait_send()
    exchange.wait_send()
    for copy in halos:
        copy.wait_recv()
    spread(1, U, 0, 0, 3)
    for copy in more:
        copy.wait_recv()
    spread(2, U, 0, 3, 3)
    finish_faces(1, copies, own)
    exchange = contact(1)
    advance(0, 4)
    out = first_sums(1, exchange)
    advance(4, BLOCKS + 8)
    second_sums(1, out)
    advance(BLOCKS + 8, 2 * BLOCKS)
    push(SLAVE, DINV[1] * SF[...])

    def store(k, block):
        copies = [
            pltpu.make_async_copy(ref.at[block], res.at[block], store_sem.at[which, k])
            for which, (ref, res) in enumerate(((U, u_out), (V, v_out)))
        ]
        for copy in copies:
            copy.start()
        return copies

    stores = store(0, (pl.ds(0, GROUPS), pl.ds(1, LAYERS - 1)))
    stores += store(1, (pl.ds(0, 2), 0)) + store(2, (pl.ds(3, 3), 0))
    force = collect_forces(1, out)
    push(MASTER, -DINV[0] * force)
    stores += store(3, (MASTER, 0))
    indices.wait_send()
    exchange.wait_send()
    for copy in out + halos + more:
        copy.wait_send()
    for copy in stores:
        copy.wait()


def body(
    n_gx, n_gy, displacement, velocity, modulus, density, clearance, mortar_coupling,
    pair_owner, pair_row, pair_offset, pair_active,
):
    owner, row, offset, active = (
        x.transpose(0, 2, 1) for x in (pair_owner, pair_row, pair_offset, pair_active)
    )
    whole = (GROUPS, LAYERS, TILE, TILE)
    hbm = pl.BlockSpec(memory_space=pl.ANY)
    vmem = pl.BlockSpec(memory_space=pltpu.VMEM)
    smem = pl.BlockSpec(memory_space=pltpu.SMEM)
    chips = n_gy // 2
    dma = pltpu.SemaphoreType.DMA
    new_disp, new_vel = pl.pallas_call(
        functools.partial(kernel, n_gx, n_gy),
        out_shape=[jax.ShapeDtypeStruct(whole, f32)] * 2,
        in_specs=[hbm] * 4 + [vmem] * 2 + [smem] * 2 + [vmem] * 4,
        out_specs=[hbm, hbm],
        scratch_shapes=[
            pltpu.VMEM(whole, f32),
            pltpu.VMEM(whole, f32),
            pltpu.VMEM((2, LAYERS, TILE, TILE), f32),
            pltpu.VMEM((2, LAYERS, TILE, TILE), f32),
            pltpu.VMEM((3, 8, LAYERS, TILE + 16, TILE), f32),
            pltpu.VMEM((BLOCKS, LAYERS, 27, 16, TILE), f32),
            pltpu.VMEM((STEPS, n_gy * TILE, TILE), f32),
            pltpu.VMEM((n_gy * TILE // 2, TILE), f32),
            pltpu.VMEM((STEPS, 2, PAIRS, TILE), f32),
            pltpu.VMEM((STEPS, chips, TILE, TILE), f32),
            pltpu.VMEM((n_gy * TILE // 2, 2 * PAIRS), jnp.bfloat16),
            pltpu.VMEM((2, 8, PAIRS), jnp.int32),
            pltpu.VMEM((2, 64, TILE), f32),
            pltpu.VMEM((2, 64, TILE), f32),
            pltpu.VMEM((4, 4, 8, TILE), f32),
            pltpu.VMEM((STEPS, 2, 64, TILE), f32),
            pltpu.VMEM((STEPS, 2, 64, TILE), f32),
            pltpu.VMEM((4, 4, 8, TILE), f32),
            pltpu.VMEM((PAIRS, TILE), jnp.int32),
            pltpu.VMEM((PAIRS, TILE), f32),
            pltpu.VMEM((PAIRS, TILE), f32),
            pltpu.VMEM((TILE, TILE), f32),
            pltpu.VMEM((PAIRS, TILE), f32),
            pltpu.VMEM((PAIRS, TILE), f32),
            pltpu.VMEM((2, TILE, TILE), f32),
            dma((4,)),
            dma((STEPS,)),
            dma((4, 8)), dma((4, 8)),
            dma((STEPS, chips)), dma((STEPS, chips)),
            dma((STEPS, chips)), dma((STEPS, chips)),
            dma((3,)), dma((3,)),
            dma((STEPS, chips)), dma((STEPS, chips)),
            dma((2, 4)),
        ],
        compiler_params=pltpu.CompilerParams(
            collective_id=0, has_side_effects=True, vmem_limit_bytes=VMEM_LIMIT
        ),
        name="impact",
    )(
        displacement.reshape(whole), velocity.reshape(whole), modulus, density,
        clearance, mortar_coupling, owner, row, owner, row, offset, active,
    )
    shape = displacement.shape
    return new_disp.reshape(shape), new_vel.reshape(shape)


def solution(mesh):
    n_gx, n_gy = mesh.shape["gx"], mesh.shape["gy"]
    nodes = P(None, None, None, "gx", "gy")
    pairs = P("gx", "gy", None)
    return jax.shard_map(
        functools.partial(body, n_gx, n_gy),
        mesh=mesh,
        in_specs=(
            nodes, nodes, P(None, None, "gx", "gy"), P(None, None, "gx", "gy"), P("gx", "gy"), P(),
            pairs, pairs, pairs, pairs,
        ),
        out_specs=(nodes, nodes),
        check_vma=False,
    )
```

```python
import functools

import jax
import jax.numpy as jnp
from jax import lax
from jax.experimental import pallas as pl
from jax.experimental.pallas import tpu as pltpu
from jax.sharding import PartitionSpec as P

STEPS = 2
LAYERS = 8
TILE = 128
BLOCKS = TILE // 8
PAIRS = 256
GROUPS = 6
MASTER, SLAVE = 2, 5
LOW, MAIN, HIGH = 7, 8, 136

time_step = 0.2
penalty_stiffness = 4.0

VMEM_LIMIT = 54 * 1024 * 1024

MESH = pl.DeviceIdType.MESH
f32 = jnp.float32


def lanes(shape):
    return lax.broadcasted_iota(jnp.int32, shape, len(shape) - 1)


def cyclic_shift(values, offsets, direction):
    for bit in range(7):
        amount = 1 << bit
        rolled = pltpu.roll(values, (direction * amount) % TILE, axis=1)
        values = jnp.where((offsets & amount) != 0, rolled, values)
    return values


def kernel(
    n_gx, n_gy,
    disp, vel, mod, dens, clear, mortar, owner_s, row_s, owner_v, row_v, offset_v, active_v,
    U, V, E, D, L, C, FACES, T, PART, RR, OH, FLAT, XS, YS, CS, HX, HY, HD, OFFS, ACT, SL, SF, ROWS, TR, DINV,
    load_sem, own_sem, halo_send, halo_recv, face_send, face_recv, pass_send, pass_recv,
    core_send, core_recv, sum_send, sum_recv,
):
    gx = lax.axis_index("gx")
    gy = lax.axis_index("gy")
    core = lax.rem(gy, 2)
    plane = n_gy // 2
    ring = n_gy // 4
    partner = gy + 1 - 2 * core
    up = lax.rem(gx + n_gx - 1, n_gx)
    down = lax.rem(gx + 1, n_gx)
    left = lax.rem(gy + n_gy - 1, n_gy)
    right = lax.rem(gy + 1, n_gy)
    other = lax.rem(gy + n_gy - 1 + 2 * core, n_gy)

    def at(x, y):
        return {"gx": x, "gy": y}

    def mate(dz, dy):
        z = lax.rem(gy // plane + dz, 2)
        y = lax.rem(lax.rem(gy, plane) // 2 + dy, ring)
        return z * plane + 2 * y + core

    loads = [
        pltpu.make_async_copy(disp, U, load_sem.at[0]),
        pltpu.make_async_copy(mod, E, load_sem.at[1]),
        pltpu.make_async_copy(dens, D, load_sem.at[2]),
        pltpu.make_async_copy(vel, V, load_sem.at[3]),
    ]
    for load in loads:
        load.start()

    barrier = pltpu.get_barrier_semaphore()
    friends = [at(gx, mate(*d)) for d in ((0, 1), (0, 2), (0, 3), (1, 0))]
    friends += [at(gx, partner), at(gx, other)]
    friends += [at(x, y) for x in (up, down) for y in (left, gy, right)]
    for friend in friends:
        pl.semaphore_signal(barrier, inc=1, device_id=friend, device_id_type=MESH)
    pl.semaphore_wait(barrier, len(friends))

    def remote(src, dst, send, recv, target):
        return pltpu.make_async_remote_copy(
            src_ref=src, dst_ref=dst, send_sem=send, recv_sem=recv,
            device_id=target, device_id_type=MESH,
        )

    def block_of(j):
        return pl.ds(pl.multiple_of(j * TILE, TILE), TILE)

    def relay(step, dz, dy, k, target):
        held = FACES.at[step, block_of(mate(dz, dy))]
        return remote(held, held, face_send.at[step, k], face_recv.at[step, k], at(gx, target))

    def send_faces(step, src):
        mine = FACES.at[step, block_of(gy)]
        copies = {}
        for k, target in ((4, mate(1, 0)), (2, mate(0, 2)), (1, mate(0, 3)), (3, mate(0, 1)), (0, partner)):
            copies[k] = remote(src, mine, face_send.at[step, k], face_recv.at[step, k], at(gx, target))
            copies[k].start()
        own = pltpu.make_async_copy(src, mine, own_sem.at[step])
        own.start()
        return copies, own

    def share(step, copies, k):
        copies[k].wait_recv()
        held = FACES.at[step, block_of(mate(k // 4, k % 4))]
        copies[8 + k] = remote(held, held, pass_send.at[step, k], pass_recv.at[step, k], at(gx, partner))
        copies[8 + k].start()

    def relay_faces(step, copies):
        share(step, copies, 4)
        copies[5] = relay(step, 1, 0, 5, mate(0, 3))
        copies[7] = relay(step, 1, 0, 7, mate(0, 1))
        copies[5].start()
        copies[7].start()
        share(step, copies, 2)
        copies[6] = relay(step, 0, 2, 6, mate(1, 0))
        copies[6].start()

    def finish_faces(step, copies, own):
        for k in (1, 3, 5, 7, 6):
            share(step, copies, k)
        own.wait()
        copies[0].wait_recv()
        for k in range(1, 8):
            copies[8 + k].wait_recv()
        for k in copies:
            copies[k].wait_send()

    def pack(phase, src, base, first, groups):
        def one(g, carry):
            lane = lanes((8, TILE))
            halves = []
            for half in range(2):
                packed = jnp.zeros((8, TILE), f32)
                for t in range(4 * BLOCKS):
                    tile = src[g - base, half * 4 + t // BLOCKS, t % BLOCKS * 8 : t % BLOCKS * 8 + 8, :]
                    packed = jnp.where(lane // 2 == t, pltpu.roll(tile, 2 * t + 1, axis=1), packed)
                halves.append(packed)
            even = lane % 2 == 0
            to_right = jnp.where(even, halves[0], pltpu.roll(halves[1], 1, axis=1))
            to_left = jnp.where(even, pltpu.roll(halves[1], TILE - 1, axis=1), halves[0])
            rows = pl.ds(pl.multiple_of(g * 8, 8), 8)
            for side, columns in enumerate((to_left, to_right)):
                YS[side, rows, :] = columns
                CS[phase, side, pl.ds(g, 1), :] = columns[0:1, :]
                CS[phase, 2 + side, pl.ds(g, 1), :] = columns[7:8, :]
            for l in range(LAYERS):
                XS[0, pl.ds(g * 8 + l, 1), :] = src[g - base, l, 0:1, :]
                XS[1, pl.ds(g * 8 + l, 1), :] = src[g - base, l, TILE - 1 : TILE, :]
            return carry

        lax.fori_loop(first, first + groups, one, 0)

    def halo_copies(phase, first, groups):
        step = 1 if phase in (1, 2) else 0
        rows = pl.ds(first * 8, groups * 8)
        plan = [
            (XS.at[0, rows], HX.at[step, 1, rows], at(up, gy)),
            (XS.at[1, rows], HX.at[step, 0, rows], at(down, gy)),
            (YS.at[0, rows], HY.at[step, 1, rows], at(gx, left)),
            (YS.at[1, rows], HY.at[step, 0, rows], at(gx, right)),
            (CS.at[phase, 0], HD.at[phase, 3], at(up, left)),
            (CS.at[phase, 1], HD.at[phase, 2], at(up, right)),
            (CS.at[phase, 2], HD.at[phase, 1], at(down, left)),
            (CS.at[phase, 3], HD.at[phase, 0], at(down, right)),
        ]
        return [
            remote(src, dst, halo_send.at[phase, k], halo_recv.at[phase, k], target)
            for k, (src, dst, target) in enumerate(plan)
        ]

    def send_halos(phase, src, base, first, groups):
        pack(phase, src, base, first, groups)
        copies = halo_copies(phase, first, groups)
        for copy in copies:
            copy.start()
        return copies

    def spread(phase, src, base, first, groups):
        step = 1 if phase in (1, 2) else 0
        at_top = (gx == 0).astype(f32)
        at_bottom = (gx == n_gx - 1).astype(f32)
        at_left = (gy == 0).astype(f32)
        at_right = (gy == n_gy - 1).astype(f32)

        def one(g, carry):
            is_mod = (g >= GROUPS).astype(f32)
            keep_top, keep_bottom = 1.0 - is_mod * at_top, 1.0 - is_mod * at_bottom
            keep_left, keep_right = 1.0 - is_mod * at_left, 1.0 - is_mod * at_right
            lane = lanes((8, TILE))
            rows = pl.ds(pl.multiple_of(g * 8, 8), 8)

            low = HY[step, 0, rows, :] * keep_left
            high = HY[step, 1, rows, :] * keep_right
            even = lane % 2 == 0
            for half in range(2):
                if half == 0:
                    both = jnp.where(even, pltpu.roll(high, TILE - 1, axis=1), pltpu.roll(low, 1, axis=1))
                else:
                    both = jnp.where(even, high, low)
                for t in range(4 * BLOCKS):
                    l = half * 4 + t // BLOCKS
                    row = t % BLOCKS * 8
                    edge = pltpu.roll(both, TILE - 1 - 2 * t, axis=1)
                    here = src[g - base, l, row : row + 8, :]
                    into = slice(MAIN + row, MAIN + row + 8)
                    L[0, g, l, into, :] = jnp.where(lane == 0, edge, pltpu.roll(here, 1, axis=1))
                    L[1, g, l, into, :] = here
                    L[2, g, l, into, :] = jnp.where(lane == TILE - 1, edge, pltpu.roll(here, TILE - 1, axis=1))
            layer = lax.broadcasted_iota(jnp.int32, (LAYERS, TILE), 0)
            upper = layer // 4

            def corner(k, block, flip):
                spot = 32 * (layer % 4) + 2 * block + (1 - upper if flip else upper)
                row = jnp.broadcast_to(HD[phase, k, pl.ds(g, 1), :], (LAYERS, TILE))
                return jnp.sum(jnp.where(lane == spot, row, 0.0), axis=1, keepdims=True)

            for side, keep, spot in ((0, keep_top, LOW), (1, keep_bottom, HIGH)):
                here = HX[step, side, rows, :] * keep
                block = 0 if side else BLOCKS - 1
                corner_low = corner(2 * side, block, False) * (keep * keep_left)
                corner_high = corner(2 * side + 1, block, True) * (keep * keep_right)
                before = pltpu.roll(jnp.where(lane == TILE - 1, corner_low, here), 1, axis=1)
                after = pltpu.roll(jnp.where(lane == 0, corner_high, here), TILE - 1, axis=1)
                for dy, plane in enumerate((before, here, after)):
                    for l in range(LAYERS):
                        L[dy, g, l, spot : spot + 1, :] = plane[l : l + 1, :]
            return carry

        lax.fori_loop(first, first + groups, one, 0)

    def couplings(first, last):
        def one(it, carry):
            b = it // (BLOCKS // 2 * LAYERS)
            t = lax.rem(it // LAYERS, BLOCKS // 2)
            l = lax.rem(it, LAYERS)
            row = pl.multiple_of(t * 16, 16)
            own = L[1, GROUPS + b, l, pl.ds(row + MAIN, 16), :]
            base = own * ((2.0 * time_step) / D[b, l, pl.ds(row, 16), :])
            total = jnp.zeros((16, TILE), f32)
            for dl in (-1, 0, 1):
                near = jnp.clip(l + dl, 0, LAYERS - 1)
                inside = jnp.logical_and(l + dl >= 0, l + dl < LAYERS).astype(f32)
                scaled = base if dl == 0 else base * inside
                weights = [scaled, scaled * 0.5, scaled * 0.25] if dl else [None, scaled, scaled * 0.5]
                for dx in (-1, 0, 1):
                    for dy in (-1, 0, 1):
                        if dl == dx == dy == 0:
                            continue
                        e = L[dy + 1, GROUPS + b, near, pl.ds(row + MAIN + dx, 16), :]
                        c = weights[abs(dx) + abs(dy)] * (e * pl.reciprocal(own + e, approx=True))
                        C[b * (BLOCKS // 2) + t, l, (dl + 1) * 9 + (dx + 1) * 3 + dy + 1] = c
                        total = total + c
            C[b * (BLOCKS // 2) + t, l, 13] = -total
            return carry

        lax.fori_loop(first, last, one, 0)

    def advance(first, last):
        def one(it, carry):
            b = it // BLOCKS
            row = pl.multiple_of(lax.rem(it, BLOCKS) * 8, 8)
            odd = pl.multiple_of(lax.rem(it, 2) * 8, 8)
            group = pl.ds(b * 3, 3)
            acc = [None] * LAYERS

            def close(l):
                v = V[group, l, pl.ds(row, 8), :] + acc[l]
                V[group, l, pl.ds(row, 8), :] = v
                U[group, l, pl.ds(row, 8), :] = U[group, l, pl.ds(row, 8), :] + time_step * v

            for l in range(LAYERS):
                for dx in (-1, 0, 1):
                    for dy in (-1, 0, 1):
                        u = L[dy + 1, group, l, pl.ds(row + MAIN + dx, 8), :]
                        for dl in (-1, 0, 1):
                            target = l - dl
                            if not 0 <= target < LAYERS:
                                continue
                            c = C[it // 2, target, (dl + 1) * 9 + (dx + 1) * 3 + dy + 1, pl.ds(odd, 8)]
                            term = c[None] * u
                            acc[target] = term if acc[target] is None else acc[target] + term
                if l > 0:
                    close(l - 1)
            close(LAYERS - 1)
            return carry

        lax.fori_loop(first, last, one, 0)

    def contact(step):
        def fetch(i, carry):
            for k in range(32):
                p = i * 32 + k
                ROWS[pl.ds(p, 1), :] = FACES[step, pl.ds(owner_s[0, 0, p] * TILE + row_s[0, 0, p], 1), :]
            return carry

        lax.fori_loop(0, PAIRS // 32, fetch, 0)
        offsets = OFFS[...]
        shifted = cyclic_shift(ROWS[...], offsets, -1)
        projected = shifted + jnp.dot(
            shifted, mortar[...], precision=lax.Precision.HIGHEST, preferred_element_type=f32
        )
        traction = ACT[...] * jnp.maximum(0.0, projected - SL[...])
        TR[...] = traction
        SF[...] = TR[pl.ds(0, TILE, stride=2), :] + TR[pl.ds(1, TILE, stride=2), :]
        back = traction + lax.dot_general(
            traction, mortar[...], (((1,), (1,)), ((), ())),
            precision=lax.Precision.HIGHEST, preferred_element_type=f32,
        )
        PART[step, 0] = cyclic_shift(back, offsets, 1)
        copy = remote(PART.at[step, 0], PART.at[step, 1], core_send.at[step], core_recv.at[step], at(gx, partner))
        copy.start()
        return copy

    order = ((1, 1), (1, 3), (1, 2), (0, 1), (0, 3), (1, 0), (0, 2), (0, 0))

    def split(values):
        coarse = values.astype(jnp.bfloat16)
        return jnp.concatenate([coarse, (values - coarse.astype(f32)).astype(jnp.bfloat16)], axis=1)

    def rows_of(there):
        return block_of(mate(*there) // 2)

    def first_sums(step, exchange):
        exchange.wait_recv()
        part = jnp.concatenate([split(PART[step, 0]), split(PART[step, 1])], axis=0)
        out = []
        for k, there in enumerate(order):
            rows = rows_of(there)
            both = jnp.dot(OH[rows, :], part, preferred_element_type=f32)
            T[rows, :] = both[:, :TILE] + both[:, TILE:]
            if k < 3:
                out.append(send_sum(step, there, k, ((0, 1), (0, 3), (1, 0))[k]))
        return out

    def late_sums(step, out):
        out.append(send_sum(step, (0, 1), 3, (0, 1)))
        out.append(send_sum(step, (0, 3), 4, (0, 3)))

    def send_sum(step, there, k, target):
        copy = remote(
            T.at[rows_of(there)], RR.at[step, k], sum_send.at[step, k], sum_recv.at[step, k],
            at(gx, mate(*target)),
        )
        copy.start()
        return copy

    def second_sums(step, out):
        out[0].wait_recv()
        out[1].wait_recv()
        rows = rows_of((1, 0))
        T[rows, :] = T[rows, :] + RR[step, 0] + RR[step, 1]
        out.append(send_sum(step, (1, 0), 5, (1, 0)))
        out[2].wait_recv()
        rows = rows_of((0, 2))
        T[rows, :] = T[rows, :] + RR[step, 2]
        out.append(send_sum(step, (0, 2), 6, (0, 2)))

    def collect_forces(step, out):
        force = T[rows_of((0, 0)), :]
        for k in (3, 4, 6, 5):
            out[k].wait_recv()
            force = force + RR[step, k]
        return force

    def push(group, force):
        v = V[group, 0] + force
        V[group, 0] = v
        U[group, 0] = U[group, 0] + time_step * force

    copies, own = send_faces(0, disp.at[MASTER, 0])
    FLAT[0] = jnp.broadcast_to(owner_v[0] * TILE + row_v[0], (8, PAIRS))
    indices = remote(FLAT.at[0], FLAT.at[1], core_send.at[2], core_recv.at[2], at(gx, partner))
    indices.start()
    loads[1].wait()
    stiff = send_halos(3, E, GROUPS, GROUPS, 2)
    loads[0].wait()
    halos = send_halos(0, U, 0, 0, GROUPS)

    OFFS[...] = jnp.broadcast_to(offset_v[0], (TILE, PAIRS)).T
    ACT[...] = penalty_stiffness * jnp.broadcast_to(active_v[0], (TILE, PAIRS)).T.astype(f32)
    indices.wait_recv()

    def hot(m, carry):
        rows = pl.ds(pl.multiple_of(m * TILE, TILE), TILE)
        index = lax.broadcasted_iota(jnp.int32, (TILE, PAIRS), 0) + (2 * m + core) * TILE
        for side in range(2):
            OH[rows, side * PAIRS : (side + 1) * PAIRS] = jnp.where(
                FLAT[side, 0:1, :] == index, 1.0, 0.0
            ).astype(jnp.bfloat16)
        return carry

    lax.fori_loop(0, n_gy // 2, hot, 0)

    def slave_gaps():
        rest = clear[...] + U[SLAVE, 0]
        SL[pl.ds(0, TILE, stride=2), :] = rest
        SL[pl.ds(1, TILE, stride=2), :] = rest

    slave_gaps()
    relay_faces(0, copies)
    for copy in stiff:
        copy.wait_recv()
    spread(3, E, GROUPS, GROUPS, 2)
    loads[2].wait()
    DINV[...] = time_step / D[:, 0]
    half = BLOCKS * LAYERS // 2
    couplings(0, half // 2)
    finish_faces(0, copies, own)
    exchange = contact(0)
    for copy in halos:
        copy.wait_recv()
    spread(0, U, 0, 0, 3)
    out = first_sums(0, exchange)
    couplings(half // 2, half)
    late_sums(0, out)
    spread(0, U, 0, 3, 3)
    loads[3].wait()
    advance(0, BLOCKS)
    second_sums(0, out)
    couplings(half, 2 * half)
    force = collect_forces(0, out)
    push(MASTER, -DINV[0] * force)

    copies, own = send_faces(1, U.at[MASTER, 0])
    for copy in halos + stiff:
        copy.wait_send()
    halos = send_halos(1, U, 0, 0, 3)
    advance(BLOCKS, BLOCKS + 14)
    relay_faces(1, copies)
    advance(BLOCKS + 14, 2 * BLOCKS)
    push(SLAVE, DINV[1] * SF[...])
    more = send_halos(2, U, 0, 3, 3)
    slave_gaps()
    for copy in out:
        copy.wait_send()
    exchange.wait_send()
    for copy in halos:
        copy.wait_recv()
    spread(1, U, 0, 0, 3)
    finish_faces(1, copies, own)
    exchange = contact(1)
    for copy in more:
        copy.wait_recv()
    spread(2, U, 0, 3, 3)
    out = first_sums(1, exchange)
    advance(0, 4)
    late_sums(1, out)
    advance(4, BLOCKS + 4)
    second_sums(1, out)
    advance(BLOCKS + 4, 2 * BLOCKS)
    push(SLAVE, DINV[1] * SF[...])

    force = collect_forces(1, out)
    push(MASTER, -DINV[0] * force)
    indices.wait_send()
    exchange.wait_send()
    for copy in out + halos + more:
        copy.wait_send()


def body(
    n_gx, n_gy, displacement, velocity, modulus, density, clearance, mortar_coupling,
    pair_owner, pair_row, pair_offset, pair_active,
):
    owner, row, offset, active = (
        x.transpose(0, 2, 1) for x in (pair_owner, pair_row, pair_offset, pair_active)
    )
    whole = (GROUPS, LAYERS, TILE, TILE)
    hbm = pl.BlockSpec(memory_space=pl.ANY)
    vmem = pl.BlockSpec(memory_space=pltpu.VMEM)
    smem = pl.BlockSpec(memory_space=pltpu.SMEM)
    chips = n_gy // 2
    dma = pltpu.SemaphoreType.DMA
    new_disp, new_vel = pl.pallas_call(
        functools.partial(kernel, n_gx, n_gy),
        out_shape=[pltpu.VMEM(whole, f32)] * 2,
        in_specs=[hbm] * 4 + [vmem] * 2 + [smem] * 2 + [vmem] * 4,
        out_specs=[vmem, vmem],
        scratch_shapes=[
            pltpu.VMEM((2, LAYERS, TILE, TILE), f32),
            pltpu.VMEM((2, LAYERS, TILE, TILE), f32),
            pltpu.VMEM((3, 8, LAYERS, TILE + 16, TILE), f32),
            pltpu.VMEM((BLOCKS, LAYERS, 27, 16, TILE), f32),
            pltpu.VMEM((STEPS, n_gy * TILE, TILE), f32),
            pltpu.VMEM((n_gy * TILE // 2, TILE), f32),
            pltpu.VMEM((STEPS, 2, PAIRS, TILE), f32),
            pltpu.VMEM((STEPS, chips, TILE, TILE), f32),
            pltpu.VMEM((n_gy * TILE // 2, 2 * PAIRS), jnp.bfloat16),
            pltpu.VMEM((2, 8, PAIRS), jnp.int32),
            pltpu.VMEM((2, 64, TILE), f32),
            pltpu.VMEM((2, 64, TILE), f32),
            pltpu.VMEM((4, 4, 8, TILE), f32),
            pltpu.VMEM((STEPS, 2, 64, TILE), f32),
            pltpu.VMEM((STEPS, 2, 64, TILE), f32),
            pltpu.VMEM((4, 4, 8, TILE), f32),
            pltpu.VMEM((PAIRS, TILE), jnp.int32),
            pltpu.VMEM((PAIRS, TILE), f32),
            pltpu.VMEM((PAIRS, TILE), f32),
            pltpu.VMEM((TILE, TILE), f32),
            pltpu.VMEM((PAIRS, TILE), f32),
            pltpu.VMEM((PAIRS, TILE), f32),
            pltpu.VMEM((2, TILE, TILE), f32),
            dma((4,)),
            dma((STEPS,)),
            dma((4, 8)), dma((4, 8)),
            dma((STEPS, chips)), dma((STEPS, chips)),
            dma((STEPS, chips)), dma((STEPS, chips)),
            dma((3,)), dma((3,)),
            dma((STEPS, chips)), dma((STEPS, chips)),
        ],
        compiler_params=pltpu.CompilerParams(
            collective_id=0, has_side_effects=True, vmem_limit_bytes=VMEM_LIMIT
        ),
        name="impact",
    )(
        displacement.reshape(whole), velocity.reshape(whole), modulus, density,
        clearance, mortar_coupling, owner, row, owner, row, offset, active,
    )
    shape = displacement.shape
    return new_disp.reshape(shape), new_vel.reshape(shape)


def solution(mesh):
    n_gx, n_gy = mesh.shape["gx"], mesh.shape["gy"]
    nodes = P(None, None, None, "gx", "gy")
    pairs = P("gx", "gy", None)
    return jax.shard_map(
        functools.partial(body, n_gx, n_gy),
        mesh=mesh,
        in_specs=(
            nodes, nodes, P(None, None, "gx", "gy"), P(None, None, "gx", "gy"), P("gx", "gy"), P(),
            pairs, pairs, pairs, pairs,
        ),
        out_specs=(nodes, nodes),
        check_vma=False,
    )
```

```python
import functools

import jax
import jax.numpy as jnp
from jax import lax
from jax.experimental import pallas as pl
from jax.experimental.pallas import tpu as pltpu
from jax.sharding import PartitionSpec as P

STEPS = 2
LAYERS = 8
TILE = 128
BLOCKS = TILE // 8
PAIRS = 256
GROUPS = 6
MASTER, SLAVE = 2, 5
LOW, MAIN, HIGH = 7, 8, 136

time_step = 0.2
penalty_stiffness = 4.0

VMEM_LIMIT = 54 * 1024 * 1024

MESH = pl.DeviceIdType.MESH
f32 = jnp.float32


def lanes(shape):
    return lax.broadcasted_iota(jnp.int32, shape, len(shape) - 1)


def cyclic_shift(values, offsets, direction):
    for bit in range(7):
        amount = 1 << bit
        rolled = pltpu.roll(values, (direction * amount) % TILE, axis=1)
        values = jnp.where((offsets & amount) != 0, rolled, values)
    return values


def kernel(
    n_gx, n_gy,
    disp, vel, mod, dens, clear, mortar, owner_s, row_s, owner_v, row_v, offset_v, active_v,
    U, V, E, D, L, C, FACES, T, PART, RR, OH, FLAT, XS, YS, CS, HX, HY, HD, OFFS, ACT, SL, SF, ROWS, TR, DINV,
    load_sem, own_sem, halo_send, halo_recv, face_send, face_recv, pass_send, pass_recv,
    core_send, core_recv, sum_send, sum_recv,
):
    gx = lax.axis_index("gx")
    gy = lax.axis_index("gy")
    core = lax.rem(gy, 2)
    plane = n_gy // 2
    ring = n_gy // 4
    partner = gy + 1 - 2 * core
    up = lax.rem(gx + n_gx - 1, n_gx)
    down = lax.rem(gx + 1, n_gx)
    left = lax.rem(gy + n_gy - 1, n_gy)
    right = lax.rem(gy + 1, n_gy)
    other = lax.rem(gy + n_gy - 1 + 2 * core, n_gy)

    def at(x, y):
        return {"gx": x, "gy": y}

    def mate(dz, dy):
        z = lax.rem(gy // plane + dz, 2)
        y = lax.rem(lax.rem(gy, plane) // 2 + dy, ring)
        return z * plane + 2 * y + core

    loads = [
        pltpu.make_async_copy(disp, U, load_sem.at[0]),
        pltpu.make_async_copy(mod, E, load_sem.at[1]),
        pltpu.make_async_copy(dens, D, load_sem.at[2]),
        pltpu.make_async_copy(vel, V, load_sem.at[3]),
    ]
    for load in loads:
        load.start()

    barrier = pltpu.get_barrier_semaphore()
    friends = [at(gx, mate(*d)) for d in ((0, 1), (0, 2), (0, 3), (1, 0))]
    friends += [at(gx, partner), at(gx, other)]
    friends += [at(x, y) for x in (up, down) for y in (left, gy, right)]
    for friend in friends:
        pl.semaphore_signal(barrier, inc=1, device_id=friend, device_id_type=MESH)
    pl.semaphore_wait(barrier, len(friends))

    def remote(src, dst, send, recv, target):
        return pltpu.make_async_remote_copy(
            src_ref=src, dst_ref=dst, send_sem=send, recv_sem=recv,
            device_id=target, device_id_type=MESH,
        )

    def block_of(j):
        return pl.ds(pl.multiple_of(j * TILE, TILE), TILE)

    def relay(step, dz, dy, k, target):
        held = FACES.at[step, block_of(mate(dz, dy))]
        return remote(held, held, face_send.at[step, k], face_recv.at[step, k], at(gx, target))

    def send_faces(step, src):
        mine = FACES.at[step, block_of(gy)]
        copies = {}
        for k, target in ((4, mate(1, 0)), (2, mate(0, 2)), (1, mate(0, 3)), (3, mate(0, 1)), (0, partner)):
            copies[k] = remote(src, mine, face_send.at[step, k], face_recv.at[step, k], at(gx, target))
            copies[k].start()
        own = pltpu.make_async_copy(src, mine, own_sem.at[step])
        own.start()
        return copies, own

    def share(step, copies, k):
        copies[k].wait_recv()
        held = FACES.at[step, block_of(mate(k // 4, k % 4))]
        copies[8 + k] = remote(held, held, pass_send.at[step, k], pass_recv.at[step, k], at(gx, partner))
        copies[8 + k].start()

    def relay_faces(step, copies):
        share(step, copies, 4)
        copies[5] = relay(step, 1, 0, 5, mate(0, 3))
        copies[7] = relay(step, 1, 0, 7, mate(0, 1))
        copies[5].start()
        copies[7].start()
        share(step, copies, 2)
        copies[6] = relay(step, 0, 2, 6, mate(1, 0))
        copies[6].start()

    def finish_faces(step, copies, own):
        for k in (1, 3, 5, 7, 6):
            share(step, copies, k)
        own.wait()
        copies[0].wait_recv()
        for k in range(1, 8):
            copies[8 + k].wait_recv()
        for k in copies:
            copies[k].wait_send()

    def pack(phase, src, base, first, groups):
        def one(g, carry):
            lane = lanes((8, TILE))
            halves = []
            for half in range(2):
                packed = jnp.zeros((8, TILE), f32)
                for t in range(4 * BLOCKS):
                    tile = src[g - base, half * 4 + t // BLOCKS, t % BLOCKS * 8 : t % BLOCKS * 8 + 8, :]
                    packed = jnp.where(lane // 2 == t, pltpu.roll(tile, 2 * t + 1, axis=1), packed)
                halves.append(packed)
            even = lane % 2 == 0
            to_right = jnp.where(even, halves[0], pltpu.roll(halves[1], 1, axis=1))
            to_left = jnp.where(even, pltpu.roll(halves[1], TILE - 1, axis=1), halves[0])
            rows = pl.ds(pl.multiple_of(g * 8, 8), 8)
            for side, columns in enumerate((to_left, to_right)):
                YS[side, rows, :] = columns
                CS[phase, side, pl.ds(g, 1), :] = columns[0:1, :]
                CS[phase, 2 + side, pl.ds(g, 1), :] = columns[7:8, :]
            for l in range(LAYERS):
                XS[0, pl.ds(g * 8 + l, 1), :] = src[g - base, l, 0:1, :]
                XS[1, pl.ds(g * 8 + l, 1), :] = src[g - base, l, TILE - 1 : TILE, :]
            return carry

        lax.fori_loop(first, first + groups, one, 0)

    def halo_copies(phase, first, groups):
        step = 1 if phase in (1, 2) else 0
        rows = pl.ds(first * 8, groups * 8)
        plan = [
            (XS.at[0, rows], HX.at[step, 1, rows], at(up, gy)),
            (XS.at[1, rows], HX.at[step, 0, rows], at(down, gy)),
            (YS.at[0, rows], HY.at[step, 1, rows], at(gx, left)),
            (YS.at[1, rows], HY.at[step, 0, rows], at(gx, right)),
            (CS.at[phase, 0], HD.at[phase, 3], at(up, left)),
            (CS.at[phase, 1], HD.at[phase, 2], at(up, right)),
            (CS.at[phase, 2], HD.at[phase, 1], at(down, left)),
            (CS.at[phase, 3], HD.at[phase, 0], at(down, right)),
        ]
        return [
            remote(src, dst, halo_send.at[phase, k], halo_recv.at[phase, k], target)
            for k, (src, dst, target) in enumerate(plan)
        ]

    def send_halos(phase, src, base, first, groups):
        pack(phase, src, base, first, groups)
        copies = halo_copies(phase, first, groups)
        for copy in copies:
            copy.start()
        return copies

    def spread(phase, src, base, first, groups):
        step = 1 if phase in (1, 2) else 0
        at_top = (gx == 0).astype(f32)
        at_bottom = (gx == n_gx - 1).astype(f32)
        at_left = (gy == 0).astype(f32)
        at_right = (gy == n_gy - 1).astype(f32)

        def one(g, carry):
            is_mod = (g >= GROUPS).astype(f32)
            keep_top, keep_bottom = 1.0 - is_mod * at_top, 1.0 - is_mod * at_bottom
            keep_left, keep_right = 1.0 - is_mod * at_left, 1.0 - is_mod * at_right
            lane = lanes((8, TILE))
            rows = pl.ds(pl.multiple_of(g * 8, 8), 8)

            low = HY[step, 0, rows, :] * keep_left
            high = HY[step, 1, rows, :] * keep_right
            even = lane % 2 == 0
            for half in range(2):
                if half == 0:
                    both = jnp.where(even, pltpu.roll(high, TILE - 1, axis=1), pltpu.roll(low, 1, axis=1))
                else:
                    both = jnp.where(even, high, low)
                for t in range(4 * BLOCKS):
                    l = half * 4 + t // BLOCKS
                    row = t % BLOCKS * 8
                    edge = pltpu.roll(both, TILE - 1 - 2 * t, axis=1)
                    here = src[g - base, l, row : row + 8, :]
                    into = slice(MAIN + row, MAIN + row + 8)
                    L[0, g, l, into, :] = jnp.where(lane == 0, edge, pltpu.roll(here, 1, axis=1))
                    L[1, g, l, into, :] = here
                    L[2, g, l, into, :] = jnp.where(lane == TILE - 1, edge, pltpu.roll(here, TILE - 1, axis=1))
            layer = lax.broadcasted_iota(jnp.int32, (LAYERS, TILE), 0)
            upper = layer // 4

            def corner(k, block, flip):
                spot = 32 * (layer % 4) + 2 * block + (1 - upper if flip else upper)
                row = jnp.broadcast_to(HD[phase, k, pl.ds(g, 1), :], (LAYERS, TILE))
                return jnp.sum(jnp.where(lane == spot, row, 0.0), axis=1, keepdims=True)

            for side, keep, spot in ((0, keep_top, LOW), (1, keep_bottom, HIGH)):
                here = HX[step, side, rows, :] * keep
                block = 0 if side else BLOCKS - 1
                corner_low = corner(2 * side, block, False) * (keep * keep_left)
                corner_high = corner(2 * side + 1, block, True) * (keep * keep_right)
                before = pltpu.roll(jnp.where(lane == TILE - 1, corner_low, here), 1, axis=1)
                after = pltpu.roll(jnp.where(lane == 0, corner_high, here), TILE - 1, axis=1)
                for dy, plane in enumerate((before, here, after)):
                    for l in range(LAYERS):
                        L[dy, g, l, spot : spot + 1, :] = plane[l : l + 1, :]
            return carry

        lax.fori_loop(first, first + groups, one, 0)

    def couplings(first, last):
        def one(it, carry):
            b = it // (BLOCKS // 2 * LAYERS)
            t = lax.rem(it // LAYERS, BLOCKS // 2)
            l = lax.rem(it, LAYERS)
            row = pl.multiple_of(t * 16, 16)
            own = L[1, GROUPS + b, l, pl.ds(row + MAIN, 16), :]
            base = own * ((2.0 * time_step) / D[b, l, pl.ds(row, 16), :])
            total = jnp.zeros((16, TILE), f32)
            for dl in (-1, 0, 1):
                near = jnp.clip(l + dl, 0, LAYERS - 1)
                inside = jnp.logical_and(l + dl >= 0, l + dl < LAYERS).astype(f32)
                scaled = base if dl == 0 else base * inside
                weights = [scaled, scaled * 0.5, scaled * 0.25] if dl else [None, scaled, scaled * 0.5]
                for dx in (-1, 0, 1):
                    for dy in (-1, 0, 1):
                        if dl == dx == dy == 0:
                            continue
                        e = L[dy + 1, GROUPS + b, near, pl.ds(row + MAIN + dx, 16), :]
                        c = weights[abs(dx) + abs(dy)] * (e * pl.reciprocal(own + e, approx=True))
                        C[b * (BLOCKS // 2) + t, l, (dl + 1) * 9 + (dx + 1) * 3 + dy + 1] = c
                        total = total + c
            C[b * (BLOCKS // 2) + t, l, 13] = -total
            return carry

        lax.fori_loop(first, last, one, 0)

    def advance(first, last):
        def one(it, carry):
            b = it // BLOCKS
            row = pl.multiple_of(lax.rem(it, BLOCKS) * 8, 8)
            odd = pl.multiple_of(lax.rem(it, 2) * 8, 8)
            group = pl.ds(b * 3, 3)
            acc = [None] * LAYERS

            def close(l):
                v = V[group, l, pl.ds(row, 8), :] + acc[l]
                V[group, l, pl.ds(row, 8), :] = v
                U[group, l, pl.ds(row, 8), :] = U[group, l, pl.ds(row, 8), :] + time_step * v

            for l in range(LAYERS):
                for dx in (-1, 0, 1):
                    for dy in (-1, 0, 1):
                        u = L[dy + 1, group, l, pl.ds(row + MAIN + dx, 8), :]
                        for dl in (-1, 0, 1):
                            target = l - dl
                            if not 0 <= target < LAYERS:
                                continue
                            c = C[it // 2, target, (dl + 1) * 9 + (dx + 1) * 3 + dy + 1, pl.ds(odd, 8)]
                            term = c[None] * u
                            acc[target] = term if acc[target] is None else acc[target] + term
                if l > 0:
                    close(l - 1)
            close(LAYERS - 1)
            return carry

        lax.fori_loop(first, last, one, 0)

    def contact(step):
        def fetch(i, carry):
            for k in range(32):
                p = i * 32 + k
                ROWS[pl.ds(p, 1), :] = FACES[step, pl.ds(owner_s[0, 0, p] * TILE + row_s[0, 0, p], 1), :]
            return carry

        lax.fori_loop(0, PAIRS // 32, fetch, 0)
        offsets = OFFS[...]
        shifted = cyclic_shift(ROWS[...], offsets, -1)
        projected = shifted + jnp.dot(
            shifted, mortar[...], precision=lax.Precision.HIGHEST, preferred_element_type=f32
        )
        traction = ACT[...] * jnp.maximum(0.0, projected - SL[...])
        TR[...] = traction
        SF[...] = TR[pl.ds(0, TILE, stride=2), :] + TR[pl.ds(1, TILE, stride=2), :]
        back = traction + lax.dot_general(
            traction, mortar[...], (((1,), (1,)), ((), ())),
            precision=lax.Precision.HIGHEST, preferred_element_type=f32,
        )
        PART[step, 0] = cyclic_shift(back, offsets, 1)
        copy = remote(PART.at[step, 0], PART.at[step, 1], core_send.at[step], core_recv.at[step], at(gx, partner))
        copy.start()
        return copy

    order = ((1, 1), (1, 3), (1, 2), (0, 1), (0, 3), (1, 0), (0, 2), (0, 0))

    def split(values):
        coarse = values.astype(jnp.bfloat16)
        return jnp.concatenate([coarse, (values - coarse.astype(f32)).astype(jnp.bfloat16)], axis=1)

    def rows_of(there):
        return block_of(mate(*there) // 2)

    def first_sums(step, exchange):
        exchange.wait_recv()
        part = jnp.concatenate([split(PART[step, 0]), split(PART[step, 1])], axis=0)
        out = []
        for k, there in enumerate(order):
            rows = rows_of(there)
            both = jnp.dot(OH[rows, :], part, preferred_element_type=f32)
            T[rows, :] = both[:, :TILE] + both[:, TILE:]
            if k < 3:
                out.append(send_sum(step, there, k, ((0, 1), (0, 3), (1, 0))[k]))
        return out

    def late_sums(step, out):
        out.append(send_sum(step, (0, 1), 3, (0, 1)))
        out.append(send_sum(step, (0, 3), 4, (0, 3)))

    def send_sum(step, there, k, target):
        copy = remote(
            T.at[rows_of(there)], RR.at[step, k], sum_send.at[step, k], sum_recv.at[step, k],
            at(gx, mate(*target)),
        )
        copy.start()
        return copy

    def second_sums(step, out):
        out[0].wait_recv()
        out[1].wait_recv()
        rows = rows_of((1, 0))
        T[rows, :] = T[rows, :] + RR[step, 0] + RR[step, 1]
        out.append(send_sum(step, (1, 0), 5, (1, 0)))
        out[2].wait_recv()
        rows = rows_of((0, 2))
        T[rows, :] = T[rows, :] + RR[step, 2]
        out.append(send_sum(step, (0, 2), 6, (0, 2)))

    def collect_forces(step, out):
        force = T[rows_of((0, 0)), :]
        for k in (3, 4, 6, 5):
            out[k].wait_recv()
            force = force + RR[step, k]
        return force

    def push(group, force):
        v = V[group, 0] + force
        V[group, 0] = v
        U[group, 0] = U[group, 0] + time_step * force

    copies, own = send_faces(0, disp.at[MASTER, 0])
    FLAT[0] = jnp.broadcast_to(owner_v[0] * TILE + row_v[0], (8, PAIRS))
    indices = remote(FLAT.at[0], FLAT.at[1], core_send.at[2], core_recv.at[2], at(gx, partner))
    indices.start()
    loads[1].wait()
    stiff = send_halos(3, E, GROUPS, GROUPS, 2)
    loads[0].wait()
    halos = send_halos(0, U, 0, 0, GROUPS)

    OFFS[...] = jnp.broadcast_to(offset_v[0], (TILE, PAIRS)).T
    ACT[...] = penalty_stiffness * jnp.broadcast_to(active_v[0], (TILE, PAIRS)).T.astype(f32)
    indices.wait_recv()

    def hot(m, carry):
        rows = pl.ds(pl.multiple_of(m * TILE, TILE), TILE)
        index = lax.broadcasted_iota(jnp.int32, (TILE, PAIRS), 0) + (2 * m + core) * TILE
        for side in range(2):
            OH[rows, side * PAIRS : (side + 1) * PAIRS] = jnp.where(
                FLAT[side, 0:1, :] == index, 1.0, 0.0
            ).astype(jnp.bfloat16)
        return carry

    def slave_gaps():
        rest = clear[...] + U[SLAVE, 0]
        SL[pl.ds(0, TILE, stride=2), :] = rest
        SL[pl.ds(1, TILE, stride=2), :] = rest

    slave_gaps()
    relay_faces(0, copies)
    for copy in stiff:
        copy.wait_recv()
    spread(3, E, GROUPS, GROUPS, 2)
    loads[2].wait()
    DINV[...] = time_step / D[:, 0]
    half = BLOCKS * LAYERS // 2
    couplings(0, half // 2)
    finish_faces(0, copies, own)
    exchange = contact(0)
    lax.fori_loop(0, n_gy // 2, hot, 0)
    out = first_sums(0, exchange)
    couplings(half // 2, half)
    late_sums(0, out)
    for copy in halos:
        copy.wait_recv()
    spread(0, U, 0, 0, GROUPS)
    loads[3].wait()
    second_sums(0, out)
    advance(0, BLOCKS)
    couplings(half, half + half // 2)
    force = collect_forces(0, out)
    push(MASTER, -DINV[0] * force)

    copies, own = send_faces(1, U.at[MASTER, 0])
    for copy in halos + stiff:
        copy.wait_send()
    halos = send_halos(1, U, 0, 0, 3)
    couplings(half + half // 2, 2 * half)
    advance(BLOCKS, BLOCKS + 8)
    relay_faces(1, copies)
    advance(BLOCKS + 8, 2 * BLOCKS)
    push(SLAVE, DINV[1] * SF[...])
    more = send_halos(2, U, 0, 3, 3)
    slave_gaps()
    for copy in out:
        copy.wait_send()
    exchange.wait_send()
    for copy in halos:
        copy.wait_recv()
    spread(1, U, 0, 0, 3)
    finish_faces(1, copies, own)
    exchange = contact(1)
    for copy in more:
        copy.wait_recv()
    spread(2, U, 0, 3, 1)
    out = first_sums(1, exchange)
    spread(2, U, 0, 4, 2)
    late_sums(1, out)
    advance(0, BLOCKS + 4)
    second_sums(1, out)
    advance(BLOCKS + 4, 2 * BLOCKS)
    push(SLAVE, DINV[1] * SF[...])

    force = collect_forces(1, out)
    push(MASTER, -DINV[0] * force)
    indices.wait_send()
    exchange.wait_send()
    for copy in out + halos + more:
        copy.wait_send()


def body(
    n_gx, n_gy, displacement, velocity, modulus, density, clearance, mortar_coupling,
    pair_owner, pair_row, pair_offset, pair_active,
):
    owner, row, offset, active = (
        x.transpose(0, 2, 1) for x in (pair_owner, pair_row, pair_offset, pair_active)
    )
    whole = (GROUPS, LAYERS, TILE, TILE)
    hbm = pl.BlockSpec(memory_space=pl.ANY)
    vmem = pl.BlockSpec(memory_space=pltpu.VMEM)
    smem = pl.BlockSpec(memory_space=pltpu.SMEM)
    chips = n_gy // 2
    dma = pltpu.SemaphoreType.DMA
    new_disp, new_vel = pl.pallas_call(
        functools.partial(kernel, n_gx, n_gy),
        out_shape=[pltpu.VMEM(whole, f32)] * 2,
        in_specs=[hbm] * 4 + [vmem] * 2 + [smem] * 2 + [vmem] * 4,
        out_specs=[vmem, vmem],
        scratch_shapes=[
            pltpu.VMEM((2, LAYERS, TILE, TILE), f32),
            pltpu.VMEM((2, LAYERS, TILE, TILE), f32),
            pltpu.VMEM((3, 8, LAYERS, TILE + 16, TILE), f32),
            pltpu.VMEM((BLOCKS, LAYERS, 27, 16, TILE), f32),
            pltpu.VMEM((STEPS, n_gy * TILE, TILE), f32),
            pltpu.VMEM((n_gy * TILE // 2, TILE), f32),
            pltpu.VMEM((STEPS, 2, PAIRS, TILE), f32),
            pltpu.VMEM((STEPS, chips, TILE, TILE), f32),
            pltpu.VMEM((n_gy * TILE // 2, 2 * PAIRS), jnp.bfloat16),
            pltpu.VMEM((2, 8, PAIRS), jnp.int32),
            pltpu.VMEM((2, 64, TILE), f32),
            pltpu.VMEM((2, 64, TILE), f32),
            pltpu.VMEM((4, 4, 8, TILE), f32),
            pltpu.VMEM((STEPS, 2, 64, TILE), f32),
            pltpu.VMEM((STEPS, 2, 64, TILE), f32),
            pltpu.VMEM((4, 4, 8, TILE), f32),
            pltpu.VMEM((PAIRS, TILE), jnp.int32),
            pltpu.VMEM((PAIRS, TILE), f32),
            pltpu.VMEM((PAIRS, TILE), f32),
            pltpu.VMEM((TILE, TILE), f32),
            pltpu.VMEM((PAIRS, TILE), f32),
            pltpu.VMEM((PAIRS, TILE), f32),
            pltpu.VMEM((2, TILE, TILE), f32),
            dma((4,)),
            dma((STEPS,)),
            dma((4, 8)), dma((4, 8)),
            dma((STEPS, chips)), dma((STEPS, chips)),
            dma((STEPS, chips)), dma((STEPS, chips)),
            dma((3,)), dma((3,)),
            dma((STEPS, chips)), dma((STEPS, chips)),
        ],
        compiler_params=pltpu.CompilerParams(
            collective_id=0, has_side_effects=True, vmem_limit_bytes=VMEM_LIMIT
        ),
        name="impact",
    )(
        displacement.reshape(whole), velocity.reshape(whole), modulus, density,
        clearance, mortar_coupling, owner, row, owner, row, offset, active,
    )
    shape = displacement.shape
    return new_disp.reshape(shape), new_vel.reshape(shape)


def solution(mesh):
    n_gx, n_gy = mesh.shape["gx"], mesh.shape["gy"]
    nodes = P(None, None, None, "gx", "gy")
    pairs = P("gx", "gy", None)
    return jax.shard_map(
        functools.partial(body, n_gx, n_gy),
        mesh=mesh,
        in_specs=(
            nodes, nodes, P(None, None, "gx", "gy"), P(None, None, "gx", "gy"), P("gx", "gy"), P(),
            pairs, pairs, pairs, pairs,
        ),
        out_specs=(nodes, nodes),
        check_vma=False,
    )
```
